256 devices in a mesh: grp: 8 (over y, core), fsdp: 32 (over x, z).
Axes of the slice: x: 4, y: 4, z: 8, core: 2. Of those that a mesh axis runs over, the one named last changes fastest.
Arguments:
- grad_part: bfloat16 [8, 8, 16, 512, 512], P('grp', None, None, 'fsdp'), may hold values from -4 to 4
- adam_v: float32 [8, 16, 512, 512], P('grp', None, 'fsdp'), may hold values from 5e-07 to 4
- owner_of: int32 [8, 16, 1], P('grp'), may hold values from 0 to 31; in each aligned block of 16 rows (0 to 15, 16 to 31, ..., all dimensions but the last counted through in order) at most 2 rows name the same one
- gram_left: float32 [8, 32, 2, 512, 512], P('grp', 'fsdp'), may hold values from -0.25 to 12
- gram_right: float32 [8, 32, 2, 512, 512], P('grp', 'fsdp'), may hold values from -0.25 to 12
- root_left: bfloat16 [8, 32, 2, 512, 512], P('grp', 'fsdp'), may hold values from -0.1 to 1.2
- root_right: bfloat16 [8, 32, 2, 512, 512], P('grp', 'fsdp'), may hold values from -0.1 to 1.2
Outputs:
- update: bfloat16 [8, 16, 512, 512], P('grp', None, 'fsdp')
- gram_left_new: float32 [8, 32, 2, 512, 512], P('grp', 'fsdp')
- gram_right_new: float32 [8, 32, 2, 512, 512], P('grp', 'fsdp')
The draws below stay inside these ranges and needn't reach their ends.
Inputs may be any that keep to these rules, and one draw needn't show every extreme that they name: `owner_of`: in each group, no owner is named by more than 2 of the group's 16 blocks, a bound that some block reaches.
All inputs are finite; a program needn't handle non-finite values.
Results may differ from the reference program's by a relative error of at most 0.022.
Values may be sent and summed in bfloat16 or wider, within the bound.
A program may use at most 64 MiB of HBM per device.

```python
import math
import jax
import jax.numpy as jnp
import numpy as np
from jax import lax

B = 512
CAP = 2
NB_ROW = 16
N_GRP = 8
N_FSDP = 32


def symmetric(noise, diagonal, spread):
    order = noise.shape[-1]
    identity = jnp.eye(order, dtype=jnp.float32)
    mirrored = 0.5 * (noise + jnp.swapaxes(noise, -1, -2))
    return spread * mirrored * (1.0 - identity) + diagonal[..., :, None] * identity


def row_ramp():
    return 1.0 + 2.0 * jnp.arange(B, dtype=jnp.float32) / (B - 1)


def draw_grad_part(key, part):
    key = jax.random.fold_in(key, 21)
    key_row, key_col, key_own = jax.random.split(key, 3)
    low = math.log(0.3)
    high = math.log(3.0)
    row_scale = jnp.exp(jax.random.uniform(key_row, (1, N_GRP, NB_ROW, B, 1), jnp.float32, low, high))
    col_scale = jnp.exp(jax.random.uniform(key_col, (1, N_GRP, NB_ROW, 1, B), jnp.float32, low, high))
    ramp = row_ramp()[:, None]
    shape = (N_GRP, N_GRP, NB_ROW, B, B)
    noise = jnp.clip(jax.random.normal(key_own, shape, jnp.float32), -5.0, 5.0)
    values = noise * row_scale * col_scale * jnp.sqrt(ramp) / math.sqrt(N_GRP * B)
    return jnp.clip(values, -4.0, 4.0).astype(jnp.bfloat16)


def draw_adam_v(key, part):
    key = jax.random.fold_in(key, 31)
    key_block, key_row, key_col, key_cell = jax.random.split(key, 4)
    shape = (N_GRP, NB_ROW, B, B)
    block_log = jax.random.uniform(key_block, (N_GRP, NB_ROW, 1, 1), jnp.float32, -1.5, 1.5)
    row_log = jax.random.uniform(key_row, (N_GRP, NB_ROW, B, 1), jnp.float32, -2.3, 2.3)
    col_log = jax.random.uniform(key_col, (N_GRP, NB_ROW, 1, B), jnp.float32, -2.3, 2.3)
    cell_log = jax.random.uniform(key_cell, shape, jnp.float32, -0.35, 0.35)
    base = 0.002
    values = base * jnp.exp(block_log + row_log + col_log + cell_log) / row_ramp()[:, None]
    return values.astype(jnp.float32)


def draw_gram_left(key, part):
    key = jax.random.fold_in(key, 11)
    key_off, key_diag = jax.random.split(key)
    shape = (N_GRP, N_FSDP, CAP, B, B)
    noise = jnp.clip(jax.random.normal(key_off, shape, jnp.float32), -4.0, 4.0)
    diagonal = jax.random.uniform(key_diag, shape[:-1], jnp.float32, 2.0, 8.0)
    return symmetric(noise, diagonal, 0.05).astype(jnp.float32)


def draw_gram_right(key, part):
    key = jax.random.fold_in(key, 12)
    key_off, key_diag = jax.random.split(key)
    shape = (N_GRP, N_FSDP, CAP, B, B)
    noise = jnp.clip(jax.random.normal(key_off, shape, jnp.float32), -4.0, 4.0)
    diagonal = jax.random.uniform(key_diag, shape[:-1], jnp.float32, 2.0, 8.0)
    return symmetric(noise, diagonal, 0.05).astype(jnp.float32)


def draw_root_left(key, part):
    key = jax.random.fold_in(key, 13)
    key_off, key_diag = jax.random.split(key)
    shape = (N_GRP, N_FSDP, CAP, B, B)
    noise = jnp.clip(jax.random.normal(key_off, shape, jnp.float32), -4.0, 4.0)
    diagonal = jax.random.uniform(key_diag, shape[:-1], jnp.float32, 0.6, 1.0)
    return symmetric(noise, diagonal, 0.015).astype(jnp.bfloat16)


def draw_root_right(key, part):
    key = jax.random.fold_in(key, 14)
    key_off, key_diag = jax.random.split(key)
    shape = (N_GRP, N_FSDP, CAP, B, B)
    noise = jnp.clip(jax.random.normal(key_off, shape, jnp.float32), -4.0, 4.0)
    diagonal = jax.random.uniform(key_diag, shape[:-1], jnp.float32, 0.6, 1.0)
    return symmetric(noise, diagonal, 0.015).astype(jnp.bfloat16)


def routed_block(key, own, number, rows, count, top, reach, lean):
    sequence = jax.random.permutation(key, count)
    packed, usual = portions_of(count, rows * top, reach, lean, True), portions_of(count, rows * top, reach, lean, False)
    places = jnp.arange(count)

    def named(lengths, offset_by):
        used = int((lengths > 0).sum())
        fixed = max(1, used // 4)
        passed = fixed + (places - fixed + offset_by * (used - fixed)) % max(1, count - fixed)
        return jnp.zeros((count,), jnp.int32).at[sequence[jnp.where(places < fixed, places, passed)]].set(jnp.asarray(lengths, jnp.int32))

    lengths = jnp.where(number % 4 == 0, named(packed, number // 4), named(usual, number - number // 4 - 1))
    mixed = jax.random.permutation(jax.random.fold_in(own, 3), count)
    donor, receiver = mixed[0:count // 2 * 2:2], mixed[1:count // 2 * 2:2]
    room = jnp.minimum(lengths[donor] - 1, reach - lengths[receiver]) // 2
    room = jnp.where((donor == sequence[0]) | (receiver == sequence[0]) | (lengths[receiver] == 0), 0, jnp.maximum(room, 0))
    passed = jax.random.randint(jax.random.fold_in(own, 4), (count // 2,), 0, 1 << 20) % (room + 1)
    lengths = lengths.at[donor].add(-passed).at[receiver].add(passed)
    labels = jnp.searchsorted(jnp.cumsum(lengths), jnp.arange(rows * top), side="right").astype(jnp.int32)
    listing = labels.reshape(top, rows).T
    listing = listing[jax.random.permutation(jax.random.fold_in(own, 1), rows)]
    offset_by = jax.random.randint(jax.random.fold_in(own, 2), (rows, 1), 0, top)
    return jnp.take_along_axis(listing, (jnp.arange(top)[None, :] + offset_by) % top, axis=1)


def portions_of(amount, total, limit, slope, full):
    loads = [(1 << 20) // math.isqrt(rank ** slope) + 1 for rank in range(1, amount + 1)]
    largest = limit if full else min(limit, max(-(-total // amount), total * loads[0] // sum(loads)))
    least = 1 if total - largest >= amount - 1 else 0
    counts, rest = [largest] + [least] * (amount - 1), total - largest - least * (amount - 1)
    while rest > 0:
        movable = [i for i in range(1, amount) if counts[i] < largest] or [i for i in range(1, amount) if counts[i] < limit]
        mass, remaining = sum([loads[i] for i in movable]), rest
        for i in movable:
            extra = min(limit - counts[i], max(1, remaining * loads[i] // mass), rest)
            counts[i] = counts[i] + extra
            rest = rest - extra
    return np.array(counts)


def setup_inputs(seed: int = 0) -> dict:
    arg_keys = jax.random.split(jax.random.key(seed), 8)
    grad_part = draw_grad_part(jax.random.fold_in(arg_keys[7], 71), 0)
    adam_v = draw_adam_v(jax.random.fold_in(arg_keys[7], 71), 0)
    owner_of_keys = jax.random.split(jax.random.fold_in(arg_keys[2], 1), N_GRP * NB_ROW // NB_ROW)
    owner_of_turns = jax.random.permutation(jax.random.fold_in(arg_keys[2], 3), N_GRP * NB_ROW // NB_ROW)
    owner_of = jax.vmap(lambda own, number: routed_block(jax.random.fold_in(arg_keys[2], 2), own, number, NB_ROW, N_FSDP, 1, CAP, 2))(owner_of_keys, owner_of_turns).reshape((N_GRP, NB_ROW, 1))
    gram_left = draw_gram_left(jax.random.fold_in(arg_keys[7], 71), 0)
    gram_right = draw_gram_right(jax.random.fold_in(arg_keys[7], 71), 0)
    root_left = draw_root_left(jax.random.fold_in(arg_keys[7], 71), 0)
    root_right = draw_root_right(jax.random.fold_in(arg_keys[7], 71), 0)
    return dict(grad_part=grad_part, adam_v=adam_v, owner_of=owner_of, gram_left=gram_left, gram_right=gram_right, root_left=root_left, root_right=root_right)


BETA2 = 0.9
EPS_ADAM = 1e-08
EPS_NORM = 1e-06
HIGHEST = lax.Precision.HIGHEST

def slot_numbers(owner_ids):
    count = owner_ids.shape[0]
    same = owner_ids[:, None] == owner_ids[None, :]
    order = jnp.arange(count, dtype=jnp.int32)
    earlier = order[None, :] < order[:, None]
    return lax.optimization_barrier(jnp.sum(jnp.where(same & earlier, 1, 0), axis=1)).astype(jnp.int32)

def one_group(replica_parts, second_old, owner_ids, left, right, left_root, right_root):
    grad_sum = lax.optimization_barrier(jnp.sum(replica_parts.astype(jnp.float32), axis=0))
    second = BETA2 * second_old + (1.0 - BETA2) * grad_sum * grad_sum
    graft_dir = grad_sum / (jnp.sqrt(second) + EPS_ADAM)
    graft_sq = lax.optimization_barrier(jnp.sum(graft_dir * graft_dir, axis=(1, 2)))
    slot_ids = slot_numbers(owner_ids)
    owner_range = jnp.arange(N_FSDP, dtype=jnp.int32)
    slot_range = jnp.arange(CAP, dtype=jnp.int32)
    select = ((owner_ids[:, None, None] == owner_range[None, :, None]) & (slot_ids[:, None, None] == slot_range[None, None, :])).astype(jnp.float32)
    outer_left = jnp.einsum('jab,jcb->jac', grad_sum, grad_sum, precision=HIGHEST)
    outer_right = jnp.einsum('jba,jbc->jac', grad_sum, grad_sum, precision=HIGHEST)
    left_new = left + jnp.einsum('jos,jac->osac', select, outer_left, precision=HIGHEST)
    right_new = right + jnp.einsum('jos,jac->osac', select, outer_right, precision=HIGHEST)
    left_pick = left_root[owner_ids, slot_ids]
    right_pick = right_root[owner_ids, slot_ids]
    grad_bf = grad_sum.astype(jnp.bfloat16)
    left_applied = jnp.einsum('jab,jbc->jac', left_pick.astype(jnp.float32), grad_bf.astype(jnp.float32)).astype(jnp.bfloat16)
    direction = jnp.einsum('jab,jbc->jac', left_applied.astype(jnp.float32), right_pick.astype(jnp.float32))
    dir_sq = lax.optimization_barrier(jnp.sum(direction * direction, axis=(1, 2)))
    scale = jnp.sqrt(graft_sq) / (jnp.sqrt(dir_sq) + EPS_NORM)
    update = (-scale[:, None, None] * direction).astype(jnp.bfloat16)
    return (update, left_new, right_new)

def reference(grad_part, adam_v, owner_of, gram_left, gram_right, root_left, root_right):
    updates = []
    lefts = []
    rights = []
    for group in range(N_GRP):
        update, left_new, right_new = one_group(grad_part[:, group], adam_v[group], owner_of[group, :, 0].astype(jnp.int32), gram_left[group], gram_right[group], root_left[group], root_right[group])
        updates.append(update)
        lefts.append(left_new)
        rights.append(right_new)
    return (jnp.stack(updates), jnp.stack(lefts), jnp.stack(rights))
```

```python
import functools

import jax
import jax.numpy as jnp
from jax import lax
from jax.experimental import pallas as pl
from jax.experimental.pallas import tpu as pltpu
from jax.sharding import PartitionSpec as P

BETA2 = 0.9
EPS_ADAM = 1e-08
EPS_NORM = 1e-06
MESH = pl.DeviceIdType.MESH

NX, NY, NZ = 4, 4, 8
BLOCKS, ROWS, ORDER, SLOTS = 16, 16, 512, 2
PARTS = 4
COLS = ORDER // PARTS
CAPS = (8,)

T_LIST, T_PLACE, T_OWNED, T_PLANE, T_RANK, T_MINE, T_HELD = 0, 64, 72, 80, 96, 112, 114


def position():
    g = lax.axis_index("grp")
    f = lax.axis_index("fsdp")
    return g, f, g // 2, g % 2, f // NZ, f % NZ


def remote(src, dst, send, recv, device):
    return pltpu.make_async_remote_copy(
        src_ref=src, dst_ref=dst, send_sem=send, recv_sem=recv,
        device_id=device, device_id_type=MESH,
    )


def pair_kernel(parts_ref, load_ref, out_ref, most_ref, own, other, loads, own_sem, send, recv, lsend, lrecv):
    g, f, y, c, x, z = position()
    own_copies = []
    for i in range(NY):
        copy = pltpu.make_async_copy(parts_ref.at[0, i * 2 + c], own.at[i], own_sem.at[i])
        copy.start()
        own_copies.append(copy)
    barrier = pltpu.get_barrier_semaphore()
    for d in range(1, 8):
        pl.semaphore_signal(barrier, inc=1, device_id=((g + d) % 8, f), device_id_type=MESH)
    pl.semaphore_wait(barrier, 7)
    load_copies = []
    for d in range(1, 8):
        copy = remote(load_ref, loads.at[d], lsend.at[d], lrecv.at[d], ((g + d) % 8, f))
        copy.start()
        load_copies.append(copy)
    copies = []
    for i in range(NY):
        copy = remote(parts_ref.at[0, i * 2 + 1 - c], other.at[i], send.at[i], recv.at[i], (y * 2 + 1 - c, f))
        copy.start()
        copies.append(copy)
    for i in range(NY):
        own_copies[i].wait()
        copies[i].wait_recv()
        for p in range(PARTS):
            cols = pl.ds(p * COLS, COLS)
            total = own[i, :, :, cols].astype(jnp.float32) + other[i, :, :, cols].astype(jnp.float32)
            out_ref[p, i] = total.astype(jnp.bfloat16)
    most = load_ref[...]
    for d in range(1, 8):
        load_copies[d - 1].wait_recv()
        most = jnp.maximum(most, loads[d])
    most_ref[...] = most
    for copy in load_copies + copies:
        copy.wait_send()


def pair_sum(grad_part, load):
    return pl.pallas_call(
        pair_kernel,
        out_shape=(
            jax.ShapeDtypeStruct((PARTS, NY, BLOCKS, ROWS, COLS), jnp.bfloat16),
            jax.ShapeDtypeStruct((8, 128), jnp.float32),
        ),
        in_specs=[pl.BlockSpec(memory_space=pl.ANY), pl.BlockSpec(memory_space=pltpu.VMEM)],
        out_specs=(pl.BlockSpec(memory_space=pltpu.VMEM), pl.BlockSpec(memory_space=pltpu.VMEM)),
        scratch_shapes=[
            pltpu.VMEM((NY, BLOCKS, ROWS, ORDER), jnp.bfloat16),
            pltpu.VMEM((NY, BLOCKS, ROWS, ORDER), jnp.bfloat16),
            pltpu.VMEM((8, 8, 128), jnp.float32),
            pltpu.SemaphoreType.DMA((NY,)),
            pltpu.SemaphoreType.DMA((NY,)),
            pltpu.SemaphoreType.DMA((NY,)),
            pltpu.SemaphoreType.DMA((8,)),
            pltpu.SemaphoreType.DMA((8,)),
        ],
        compiler_params=pltpu.CompilerParams(
            collective_id=0, has_side_effects=True, vmem_limit_bytes=32 << 20
        ),
        name="pair_sum",
    )(grad_part, load)


def step_kernel(cap, tbl, pairs, adam_hbm, gl_hbm, gr_hbm, rl_hbm, rr_hbm,
                upd, gl_out, gr_out, *scratch):
    scratch = list(scratch)
    take = lambda n: [scratch.pop(0) for _ in range(n)]
    gbf, zsend, zrecv, xret, zback, zret = (take(PARTS) for _ in range(6))
    (yown, yrecv, gsum, xsend, xrecv, gmat, dirb, xback, adam, gl, gr, rl, rr,
     gpart, gzrecv, gzsum, gxrecv,
     lsem, ysem, ysend_sem, yrecv_sem, zsend_sem, zrecv_sem, xsend_sem, xrecv_sem,
     bxsend_sem, bxrecv_sem, bzsend_sem, bzrecv_sem, gsend_sem, grecv_sem, osem) = scratch
    g, f, y, c, x, z = position()
    at_y = lambda i: (i * 2 + c, f)
    at_z = lambda i: (g, x * NZ + i)
    at_x = lambda i: (g, i * NZ + z)
    plus = lambda a, d, n: (a + d) % n
    sends = []

    def start(copy):
        copy.start()
        sends.append(copy)
        return copy

    own_copies = []
    for p in range(PARTS):
        copy = pltpu.make_async_copy(pairs.at[p, y], yown.at[p], ysem.at[p])
        copy.start()
        own_copies.append(copy)
    big = []
    for i, (src, dst) in enumerate(((adam_hbm.at[0], adam), (rl_hbm.at[0, 0], rl), (rr_hbm.at[0, 0], rr),
                                    (gl_hbm.at[0, 0], gl), (gr_hbm.at[0, 0], gr))):
        copy = pltpu.make_async_copy(src, dst, lsem.at[i])
        copy.start()
        big.append(copy)

    barrier = pltpu.get_barrier_semaphore()
    partners = (
        [at_y(plus(y, d, NY)) for d in range(1, NY)]
        + [at_z(plus(z, d, NZ)) for d in range(1, NZ)]
        + [at_x(plus(x, d, NX)) for d in range(1, NX)]
    )
    for partner in partners:
        pl.semaphore_signal(barrier, inc=1, device_id=partner, device_id_type=MESH)
    pl.semaphore_wait(barrier, len(partners))

    y_copies = [[] for _ in range(PARTS)]
    for p in range(PARTS):
        for d in range(1, NY):
            to = plus(y, d, NY)
            y_copies[p].append(start(remote(
                pairs.at[p, to], yrecv.at[p, d - 1], ysend_sem.at[p * 3 + d - 1], yrecv_sem.at[p * 3 + d - 1], at_y(to))))

    z_copies = [[] for _ in range(PARTS)]
    x_copies = [[] for _ in range(PARTS)]
    bx_copies = [[] for _ in range(PARTS)]
    bz_copies = [[] for _ in range(PARTS)]

    def reduce_part(p):
        own_copies[p].wait()
        for copy in y_copies[p]:
            copy.wait_recv()
        total = yown[p].astype(jnp.float32)
        for d in range(NY - 1):
            total = total + yrecv[p, d].astype(jnp.float32)
        gsum[p] = total
        gbf[p][...] = total.astype(jnp.bfloat16)

        @pl.loop(0, NZ)
        def _(i):
            for k in range(cap):
                zsend[p][i, k] = gbf[p][tbl[T_LIST + i * 8 + k]]

        for d in range(1, NZ):
            to = plus(z, d, NZ)
            n = p * 7 + d - 1
            z_copies[p].append(start(remote(
                zsend[p].at[to], zrecv[p].at[z], zsend_sem.at[n], zrecv_sem.at[n], at_z(to))))
        zrecv[p][z] = zsend[p][z]

    def pass_on(p):
        for copy in z_copies[p]:
            copy.wait_recv()

        for i in range(NX * SLOTS):
            k = tbl[T_PLACE + i]
            for r in range(NZ):
                xsend[p, i // SLOTS, i % SLOTS, r] = zrecv[p][r, k]

        for d in range(1, NX):
            to = plus(x, d, NX)
            n = p * 3 + d - 1
            x_copies[p].append(start(remote(
                xsend.at[p, to], xrecv.at[p, x], xsend_sem.at[n], xrecv_sem.at[n], at_x(to))))
        xrecv[p, x] = xsend[p, x]

    def apply_roots(p):
        for copy in x_copies[p]:
            copy.wait_recv()

        @pl.loop(0, SLOTS)
        def _(s):
            block = xrecv[p, :, s].reshape(ORDER, COLS)
            gmat[s, :, p * COLS:(p + 1) * COLS] = block
            left = jnp.dot(rl[s], block, preferred_element_type=jnp.float32).astype(jnp.bfloat16)
            term = jnp.dot(left, rr[s, p * COLS:(p + 1) * COLS, :], preferred_element_type=jnp.float32)
            if p == 0:
                dirb[s] = term
            else:
                dirb[s] += term

    graft_z = []
    graft_x = []

    def graft_first():
        big[0].wait()
        part = jnp.zeros((BLOCKS, COLS), jnp.float32)
        for p in range(PARTS):
            total = gsum[p]
            second = BETA2 * adam[:, :, p * COLS:(p + 1) * COLS] + (1.0 - BETA2) * total * total
            ratio = total / (jnp.sqrt(second) + EPS_ADAM)
            part = part + jnp.sum(ratio * ratio, axis=1)
        gpart[...] = part
        for d in range(1, NZ):
            graft_z.append(start(remote(
                gpart, gzrecv.at[d - 1], gsend_sem.at[d - 1], grecv_sem.at[d - 1], at_z(plus(z, d, NZ)))))

    def graft_second():
        total = gpart[...]
        for d in range(NZ - 1):
            graft_z[d].wait_recv()
            total = total + gzrecv[d]
        gzsum[...] = total
        for d in range(1, NX):
            n = 6 + d
            graft_x.append(start(remote(
                gzsum, gxrecv.at[d - 1], gsend_sem.at[n], grecv_sem.at[n], at_x(plus(x, d, NX)))))

    reduce_part(0)
    reduce_part(1)
    pass_on(0)
    reduce_part(2)
    pass_on(1)
    reduce_part(3)
    graft_first()
    big[1].wait()
    big[2].wait()
    apply_roots(0)
    pass_on(2)
    graft_second()
    apply_roots(1)
    pass_on(3)
    apply_roots(2)
    graft = gzsum[...]
    for d in range(NX - 1):
        graft_x[d].wait_recv()
        graft = graft + gxrecv[d]
    block_ids = lax.broadcasted_iota(jnp.int32, (BLOCKS, COLS), 0)
    graft_norms = []
    for s in range(SLOTS):
        graft_norms.append(jnp.sqrt(jnp.sum(jnp.where(block_ids == tbl[T_MINE + s], graft, 0.0), keepdims=True)))
    apply_roots(3)

    for s in range(SLOTS):
        whole = dirb[s]
        norm = jnp.sqrt(jnp.sum(whole * whole, keepdims=True))
        scale = -(graft_norms[s] / (norm + EPS_NORM))
        for p in range(PARTS):
            piece = (whole[:, p * COLS:(p + 1) * COLS] * scale).astype(jnp.bfloat16)
            xback[p, :, s] = piece.reshape(NX, NZ, ROWS, COLS)
    for p in range(PARTS):
        for d in range(1, NX):
            to = plus(x, d, NX)
            n = p * 3 + d - 1
            bx_copies[p].append(start(remote(
                xback.at[p, to], xret[p].at[x], bxsend_sem.at[n], bxrecv_sem.at[n], at_x(to))))
        xret[p][x] = xback[p, x]

    big[3].wait()
    big[4].wait()

    @pl.loop(0, SLOTS)
    def _(s):
        held = tbl[T_HELD + s] > 0
        block = gmat[s]
        outer = lax.dot_general(block, block, (((1,), (1,)), ((), ())), preferred_element_type=jnp.float32)
        gl[s] = gl[s] + jnp.where(held, outer, 0.0)
        outer = lax.dot_general(block, block, (((0,), (0,)), ((), ())), preferred_element_type=jnp.float32)
        gr[s] = gr[s] + jnp.where(held, outer, 0.0)

    out_copies = [
        pltpu.make_async_copy(gl, gl_out.at[0, 0], osem.at[0]),
        pltpu.make_async_copy(gr, gr_out.at[0, 0], osem.at[1]),
    ]
    for copy in out_copies:
        copy.start()

    def pass_back(p):
        for copy in bx_copies[p]:
            copy.wait_recv()

        for k in range(cap):
            e = tbl[T_OWNED + k]
            for r in range(NZ):
                zback[p][r, k] = xret[p][e // SLOTS, e % SLOTS, r]

        for d in range(1, NZ):
            to = plus(z, d, NZ)
            n = p * 7 + d - 1
            bz_copies[p].append(start(remote(
                zback[p].at[to], zret[p].at[z], bzsend_sem.at[n], bzrecv_sem.at[n], at_z(to))))
        zret[p][z] = zback[p][z]

    def finish(p):
        for copy in bz_copies[p]:
            copy.wait_recv()
        for j in range(BLOCKS):
            upd[0, j, :, p * COLS:(p + 1) * COLS] = zret[p][tbl[T_PLANE + j], tbl[T_RANK + j]]

    for p in range(PARTS):
        pass_back(p)
    for p in range(PARTS):
        finish(p)
    for copy in out_copies:
        copy.wait()
    for copy in sends:
        copy.wait_send()


def step(cap, collective_id, tbl, pairs, adam_v, gram_left, gram_right, root_left, root_right):
    tile = (ROWS, COLS)
    bf, f32 = jnp.bfloat16, jnp.float32
    vm = pltpu.VMEM
    dma = pltpu.SemaphoreType.DMA
    scratch = (
        [vm((BLOCKS,) + tile, bf)] * PARTS
        + [vm((NZ, cap) + tile, bf)] * PARTS
        + [vm((NZ, cap) + tile, bf)] * PARTS
        + [vm((NX, SLOTS, NZ) + tile, bf)] * PARTS
        + [vm((NZ, cap) + tile, bf)] * PARTS
        + [vm((NZ, cap) + tile, bf)] * PARTS
        + [
            vm((PARTS, BLOCKS) + tile, bf),
            vm((PARTS, NY - 1, BLOCKS) + tile, bf),
            vm((PARTS, BLOCKS) + tile, f32),
            vm((PARTS, NX, SLOTS, NZ) + tile, bf),
            vm((PARTS, NX, SLOTS, NZ) + tile, bf),
            vm((SLOTS, ORDER, ORDER), bf),
            vm((SLOTS, ORDER, ORDER), f32),
            vm((PARTS, NX, SLOTS, NZ) + tile, bf),
            vm((BLOCKS, ROWS, ORDER), f32),
            vm((SLOTS, ORDER, ORDER), f32),
            vm((SLOTS, ORDER, ORDER), f32),
            vm((SLOTS, ORDER, ORDER), bf),
            vm((SLOTS, ORDER, ORDER), bf),
            vm((BLOCKS, COLS), f32),
            vm((NZ - 1, BLOCKS, COLS), f32),
            vm((BLOCKS, COLS), f32),
            vm((NX - 1, BLOCKS, COLS), f32),
            dma((5,)), dma((PARTS,)),
            dma((PARTS * 3,)), dma((PARTS * 3,)),
            dma((PARTS * 7,)), dma((PARTS * 7,)),
            dma((PARTS * 3,)), dma((PARTS * 3,)),
            dma((PARTS * 3,)), dma((PARTS * 3,)),
            dma((PARTS * 7,)), dma((PARTS * 7,)),
            dma((10,)), dma((10,)), dma((2,)),
        ]
    )
    hbm = pl.BlockSpec(memory_space=pl.ANY)
    return pl.pallas_call(
        functools.partial(step_kernel, cap),
        out_shape=(
            jax.ShapeDtypeStruct((1, BLOCKS, ROWS, ORDER), bf),
            jax.ShapeDtypeStruct(gram_left.shape, f32),
            jax.ShapeDtypeStruct(gram_right.shape, f32),
        ),
        in_specs=[pl.BlockSpec(memory_space=pltpu.SMEM)] + [hbm] * 6,
        out_specs=(pl.BlockSpec(memory_space=pltpu.VMEM), hbm, hbm),
        scratch_shapes=scratch,
        compiler_params=pltpu.CompilerParams(
            collective_id=collective_id, has_side_effects=True, vmem_limit_bytes=48 << 20
        ),
        name=f"step_{cap}",
    )(tbl, pairs, adam_v, gram_left, gram_right, root_left, root_right)


def index_table(owner_ids):
    me = lax.axis_index("fsdp")
    iota = lambda n: jnp.arange(n, dtype=jnp.int32)
    order = iota(BLOCKS)
    earlier = order[None, :] < order[:, None]
    plane, line = owner_ids % NZ, owner_ids // NZ
    count = lambda same: jnp.sum(jnp.where(same & earlier, 1, 0), axis=1).astype(jnp.int32)
    slot = count(owner_ids[:, None] == owner_ids[None, :])
    rank = count(plane[:, None] == plane[None, :])
    pick = lambda where, value: jnp.sum(jnp.where(where, value, 0), axis=-1).astype(jnp.int32).reshape(-1)
    listed = pick((plane == iota(NZ)[:, None, None]) & (rank == iota(8)[None, :, None]), order)
    owners = iota(NX)[:, None, None] * NZ + me % NZ
    place = pick((owner_ids == owners) & (slot == iota(SLOTS)[None, :, None]), rank)
    owned = pick((plane == me % NZ) & (rank == iota(8)[:, None]), line * SLOTS + slot)
    is_mine = (owner_ids == me) & (slot == iota(SLOTS)[:, None])
    mine = pick(is_mine, order)
    held = pick(is_mine, 1)
    table = jnp.concatenate([listed, place, owned, plane, rank, mine, held, jnp.zeros((12,), jnp.int32)])
    return table, jnp.max(rank) + 1


def per_device(grad_part, adam_v, owner_of, gram_left, gram_right, root_left, root_right):
    table, load = index_table(owner_of[0, :, 0])
    load = jnp.broadcast_to(load.astype(jnp.float32), (8, 128))
    pairs, most = pair_sum(grad_part, load)
    operands = (table, pairs, adam_v, gram_left, gram_right, root_left, root_right)
    if len(CAPS) == 1:
        return step(CAPS[0], 1, *operands)
    most = most[0, 0]
    which = sum((most > cap).astype(jnp.int32) for cap in CAPS[:-1])
    branches = [functools.partial(step, cap, i + 1) for i, cap in enumerate(CAPS)]
    return lax.switch(which, branches, *operands)


def solution(mesh):
    placed = (
        P("grp", None, None, "fsdp", None),
        P("grp", None, "fsdp", None),
        P("grp", None, None),
        P("grp", "fsdp", None, None, None),
        P("grp", "fsdp", None, None, None),
        P("grp", "fsdp", None, None, None),
        P("grp", "fsdp", None, None, None),
    )
    return jax.shard_map(
        per_device,
        mesh=mesh,
        in_specs=placed,
        out_specs=(
            P("grp", None, "fsdp", None),
            P("grp", "fsdp", None, None, None),
            P("grp", "fsdp", None, None, None),
        ),
        check_vma=False,
    )
```

```python
import functools

import jax
import jax.numpy as jnp
from jax import lax
from jax.experimental import pallas as pl
from jax.experimental.pallas import tpu as pltpu
from jax.sharding import PartitionSpec as P

BETA2 = 0.9
EPS_ADAM = 1e-08
EPS_NORM = 1e-06
MESH = pl.DeviceIdType.MESH

NX, NY, NZ = 4, 4, 8
BLOCKS, ROWS, ORDER, SLOTS = 16, 16, 512, 2
PARTS = 4
COLS = ORDER // PARTS
CAPS = (4, 5, 8)
CHUNKS = 4
BACK_ORDER = (4, 3, 5, 2, 6, 1, 7, 0)

T_LIST, T_PLACE, T_OWNED, T_PLANE, T_RANK, T_MINE, T_HELD = 0, 64, 72, 80, 96, 112, 114


def position():
    g = lax.axis_index("grp")
    f = lax.axis_index("fsdp")
    return g, f, g // 2, g % 2, f // NZ, f % NZ


def remote(src, dst, send, recv, device):
    return pltpu.make_async_remote_copy(
        src_ref=src, dst_ref=dst, send_sem=send, recv_sem=recv,
        device_id=device, device_id_type=MESH,
    )


def index_table(owner_ref, me, z):
    shape = (BLOCKS, 128)
    row = lax.broadcasted_iota(jnp.int32, shape, 0)
    lane = lax.broadcasted_iota(jnp.int32, shape, 1)
    down = jnp.zeros(shape, jnp.int32)
    across = jnp.zeros(shape, jnp.int32)
    for j in range(BLOCKS):
        down = jnp.where(row == j, owner_ref[j], down)
        across = jnp.where(lane == j, owner_ref[j], across)
    count = lambda same: jnp.sum(jnp.where(same & (lane < row), 1.0, 0.0), axis=1, keepdims=True)
    slot = count(down == across).astype(jnp.int32)
    ranks = count(down % NZ == across % NZ)
    rank = ranks.astype(jnp.int32)
    plane, line = down % NZ, down // NZ
    here = plane == z
    mine = down == me
    whole = jnp.zeros(shape, jnp.int32)
    for first, size, cond, value in (
        (T_LIST, 64, lambda e: (plane == e // 8) & (rank == e % 8), row),
        (T_PLACE, 8, lambda e: here & (line == e // SLOTS) & (slot == e % SLOTS), rank),
        (T_OWNED, 8, lambda e: here & (rank == e), line * SLOTS + slot),
        (T_PLANE, 16, lambda e: row == e, plane),
        (T_RANK, 16, lambda e: row == e, rank),
        (T_MINE, 2, lambda e: mine & (slot == e), row),
        (T_HELD, 2, lambda e: mine & (slot == e), 1),
    ):
        entry = lane - first
        whole += jnp.where((entry >= 0) & (entry < size) & cond(entry), value, 0)
    table = jnp.sum(whole.astype(jnp.float32), axis=0, keepdims=True).astype(jnp.int32)
    return table, jnp.max(ranks, keepdims=True) + 1.0


def pair_kernel(parts_ref, owner_ref, out_ref, tbl_ref, which_ref,
                own, other, load, loads, own_sem, send, recv, lsend, lrecv):
    g, f, y, c, x, z = position()
    own_copies = []
    for i in range(NY):
        copy = pltpu.make_async_copy(parts_ref.at[0, i * 2 + c], own.at[i], own_sem.at[i])
        copy.start()
        own_copies.append(copy)
    barrier = pltpu.get_barrier_semaphore()
    for d in range(1, 8):
        pl.semaphore_signal(barrier, inc=1, device_id=((g + d) % 8, f), device_id_type=MESH)
    table, most = index_table(owner_ref, f, z)
    tbl_ref[...] = jnp.broadcast_to(table, (8, 128))
    load[...] = jnp.broadcast_to(most, (8, 128))
    pl.semaphore_wait(barrier, 7)
    copies = []
    for i in range(NY):
        copy = remote(parts_ref.at[0, i * 2 + 1 - c], other.at[i], send.at[i], recv.at[i], (y * 2 + 1 - c, f))
        copy.start()
        copies.append(copy)
    load_copies = []
    for d in range(1, 8):
        copy = remote(load, loads.at[d], lsend.at[d], lrecv.at[d], ((g + d) % 8, f))
        copy.start()
        load_copies.append(copy)
    for i in range(NY):
        own_copies[i].wait()
        copies[i].wait_recv()
        for p in range(PARTS):
            cols = pl.ds(p * COLS, COLS)
            total = own[i, :, :, cols].astype(jnp.float32) + other[i, :, :, cols].astype(jnp.float32)
            out_ref[p, i] = total.astype(jnp.bfloat16)
    most = load[...]
    for d in range(1, 8):
        load_copies[d - 1].wait_recv()
        most = jnp.maximum(most, loads[d])
    most = jnp.max(most)
    which_ref[0] = sum((most > cap).astype(jnp.int32) for cap in CAPS[:-1])
    for copy in load_copies + copies:
        copy.wait_send()


def pair_sum(grad_part, owner_ids):
    return pl.pallas_call(
        pair_kernel,
        out_shape=(
            jax.ShapeDtypeStruct((PARTS, NY, BLOCKS, ROWS, COLS), jnp.bfloat16),
            jax.ShapeDtypeStruct((8, 128), jnp.int32),
            jax.ShapeDtypeStruct((1,), jnp.int32),
        ),
        in_specs=[pl.BlockSpec(memory_space=pl.ANY), pl.BlockSpec(memory_space=pltpu.SMEM)],
        out_specs=(
            pl.BlockSpec(memory_space=pltpu.VMEM),
            pl.BlockSpec(memory_space=pltpu.VMEM),
            pl.BlockSpec(memory_space=pltpu.SMEM),
        ),
        scratch_shapes=[
            pltpu.VMEM((NY, BLOCKS, ROWS, ORDER), jnp.bfloat16),
            pltpu.VMEM((NY, BLOCKS, ROWS, ORDER), jnp.bfloat16),
            pltpu.VMEM((8, 128), jnp.float32),
            pltpu.VMEM((8, 8, 128), jnp.float32),
            pltpu.SemaphoreType.DMA((NY,)),
            pltpu.SemaphoreType.DMA((NY,)),
            pltpu.SemaphoreType.DMA((NY,)),
            pltpu.SemaphoreType.DMA((8,)),
            pltpu.SemaphoreType.DMA((8,)),
        ],
        compiler_params=pltpu.CompilerParams(
            collective_id=0, has_side_effects=True, vmem_limit_bytes=60 << 20
        ),
        name="pair_sum",
    )(grad_part, owner_ids)


def step_kernel(cap, tbl_hbm, pairs, adam_hbm, gl_hbm, gr_hbm, rl_hbm, rr_hbm,
                upd, gl_out, gr_out, *scratch):
    scratch = list(scratch)
    take = lambda n: [scratch.pop(0) for _ in range(n)]
    gbf, zsend, zrecv = (take(PARTS) for _ in range(3))
    xret = take(NZ)
    (yown, yrecv, gsum, xsend, xrecv, gmat, dirb, xback, zback, zret, adam, gl, gr, rl, rr,
     gpart, gzrecv, gzsum, gxrecv, tbls,
     lsem, ysem, ysend_sem, yrecv_sem, zsend_sem, zrecv_sem, xsend_sem, xrecv_sem,
     bxsend_sem, bxrecv_sem, bzsend_sem, bzrecv_sem, gsend_sem, grecv_sem, osem) = scratch
    g, f, y, c, x, z = position()
    at_y = lambda i: (i * 2 + c, f)
    at_z = lambda i: (g, x * NZ + i)
    at_x = lambda i: (g, i * NZ + z)
    plus = lambda a, d, n: (a + d) % n
    sends = []

    def start(copy):
        copy.start()
        sends.append(copy)
        return copy

    own_copies = []
    for p in range(PARTS):
        copy = pltpu.make_async_copy(pairs.at[p, y], yown.at[p], ysem.at[p])
        copy.start()
        own_copies.append(copy)
    big = []
    for i, (src, dst) in enumerate(((adam_hbm.at[0], adam), (rl_hbm.at[0, 0], rl), (rr_hbm.at[0, 0], rr),
                                    (gl_hbm.at[0, 0], gl), (gr_hbm.at[0, 0], gr), (tbl_hbm, tbls))):
        copy = pltpu.make_async_copy(src, dst, lsem.at[i])
        copy.start()
        big.append(copy)

    barrier = pltpu.get_barrier_semaphore()
    partners = (
        [at_y(plus(y, d, NY)) for d in range(1, NY)]
        + [at_z(plus(z, d, NZ)) for d in range(1, NZ)]
        + [at_x(plus(x, d, NX)) for d in range(1, NX)]
    )
    for partner in partners:
        pl.semaphore_signal(barrier, inc=1, device_id=partner, device_id_type=MESH)
    pl.semaphore_wait(barrier, len(partners))

    y_copies = [[] for _ in range(PARTS)]
    for p in range(PARTS):
        for d in range(1, NY):
            to = plus(y, d, NY)
            y_copies[p].append(start(remote(
                pairs.at[p, to], yrecv.at[p, d - 1], ysend_sem.at[p * 3 + d - 1], yrecv_sem.at[p * 3 + d - 1], at_y(to))))

    z_copies = [[] for _ in range(PARTS)]
    x_copies = [[] for _ in range(PARTS)]

    def tbl(i):
        return tbls[0, i]

    def reduce_part(p):
        own_copies[p].wait()
        for copy in y_copies[p]:
            copy.wait_recv()
        total = yown[p].astype(jnp.float32)
        for d in range(NY - 1):
            total = total + yrecv[p, d].astype(jnp.float32)
        gsum[p] = total
        gbf[p][...] = total.astype(jnp.bfloat16)

        @pl.loop(0, NZ)
        def _(i):
            for k in range(cap):
                zsend[p][i, k] = gbf[p][tbl(T_LIST + i * 8 + k)]

        for d in range(1, NZ):
            to = plus(z, d, NZ)
            n = p * 7 + d - 1
            z_copies[p].append(start(remote(
                zsend[p].at[to], zrecv[p].at[z], zsend_sem.at[n], zrecv_sem.at[n], at_z(to))))
        zrecv[p][z] = zsend[p][z]

    def pass_on(p):
        for copy in z_copies[p]:
            copy.wait_recv()

        for i in range(NX * SLOTS):
            k = tbl(T_PLACE + i)
            for r in range(NZ):
                xsend[p, i // SLOTS, i % SLOTS, r] = zrecv[p][r, k]

        for d in range(1, NX):
            to = plus(x, d, NX)
            n = p * 3 + d - 1
            x_copies[p].append(start(remote(
                xsend.at[p, to], xrecv.at[p, x], xsend_sem.at[n], xrecv_sem.at[n], at_x(to))))
        xrecv[p, x] = xsend[p, x]

    def apply_roots(p):
        for copy in x_copies[p]:
            copy.wait_recv()

        @pl.loop(0, SLOTS)
        def _(s):
            block = xrecv[p, :, s].reshape(ORDER, COLS)
            gmat[s, :, p * COLS:(p + 1) * COLS] = block
            left = jnp.dot(rl[s], block, preferred_element_type=jnp.float32).astype(jnp.bfloat16)
            term = jnp.dot(left, rr[s, p * COLS:(p + 1) * COLS, :], preferred_element_type=jnp.float32)
            if p == 0:
                dirb[s] = term
            else:
                dirb[s] += term

    graft_z = []
    graft_x = []

    def graft_first():
        big[0].wait()
        part = jnp.zeros((BLOCKS, COLS), jnp.float32)
        for p in range(PARTS):
            total = gsum[p]
            second = BETA2 * adam[:, :, p * COLS:(p + 1) * COLS] + (1.0 - BETA2) * total * total
            ratio = total / (jnp.sqrt(second) + EPS_ADAM)
            part = part + jnp.sum(ratio * ratio, axis=1)
        gpart[...] = part
        for d in range(1, NZ):
            graft_z.append(start(remote(
                gpart, gzrecv.at[d - 1], gsend_sem.at[d - 1], grecv_sem.at[d - 1], at_z(plus(z, d, NZ)))))

    def graft_second():
        total = gpart[...]
        for d in range(NZ - 1):
            graft_z[d].wait_recv()
            total = total + gzrecv[d]
        gzsum[...] = total
        for d in range(1, NX):
            n = 6 + d
            graft_x.append(start(remote(
                gzsum, gxrecv.at[d - 1], gsend_sem.at[n], grecv_sem.at[n], at_x(plus(x, d, NX)))))

    big[5].wait()
    reduce_part(0)
    reduce_part(1)
    pass_on(0)
    reduce_part(2)
    pass_on(1)
    reduce_part(3)
    graft_first()
    big[1].wait()
    big[2].wait()
    apply_roots(0)
    pass_on(2)
    graft_second()
    apply_roots(1)
    pass_on(3)
    apply_roots(2)
    graft = gzsum[...]
    for d in range(NX - 1):
        graft_x[d].wait_recv()
        graft = graft + gxrecv[d]
    block_ids = lax.broadcasted_iota(jnp.int32, (BLOCKS, COLS), 0)
    graft_norms = []
    for s in range(SLOTS):
        graft_norms.append(jnp.sqrt(jnp.sum(jnp.where(block_ids == tbl(T_MINE + s), graft, 0.0), keepdims=True)))
    apply_roots(3)

    for s in range(SLOTS):
        whole = dirb[s]
        norm = jnp.sqrt(jnp.sum(whole * whole, keepdims=True))
        scale = -(graft_norms[s] / (norm + EPS_NORM))
        xback[:, s] = (whole * scale).astype(jnp.bfloat16).reshape(NX, NZ, ROWS, ORDER)
    bx_copies = [[] for _ in range(NZ)]
    bz_copies = []
    for d in BACK_ORDER:
        plane = plus(z, d, NZ)
        for e in range(1, NX):
            to = plus(x, e, NX)
            n = d * 3 + e - 1
            bx_copies[d].append(start(remote(
                xback.at[to, :, plane], xret[d].at[x], bxsend_sem.at[n], bxrecv_sem.at[n], at_x(to))))
        xret[d][x] = xback[x, :, plane]

    big[3].wait()
    big[4].wait()

    @pl.loop(0, SLOTS)
    def _(s):
        held = tbl(T_HELD + s) > 0
        block = gmat[s]
        outer = lax.dot_general(block, block, (((1,), (1,)), ((), ())), preferred_element_type=jnp.float32)
        gl_out[0, 0, s] = gl[s] + jnp.where(held, outer, 0.0)
        outer = lax.dot_general(block, block, (((0,), (0,)), ((), ())), preferred_element_type=jnp.float32)
        gr[s] = gr[s] + jnp.where(held, outer, 0.0)

    out_copy = pltpu.make_async_copy(gr, gr_out.at[0, 0], osem)
    out_copy.start()

    for d in BACK_ORDER:
        for copy in bx_copies[d]:
            copy.wait_recv()
        land = zback if d else zret
        for k in range(cap):
            e = tbl(T_OWNED + k)
            land[d, k] = xret[d][e // SLOTS, e % SLOTS]
        if d:
            bz_copies.append(start(remote(
                zback.at[d], zret.at[d], bzsend_sem.at[d - 1], bzrecv_sem.at[d - 1], at_z(plus(z, d, NZ)))))
    for copy in bz_copies:
        copy.wait_recv()
    for j in range(BLOCKS):
        away = (z + NZ - tbl(T_PLANE + j)) % NZ
        upd[0, j] = zret[away, tbl(T_RANK + j)]
    out_copy.wait()
    for copy in sends:
        copy.wait_send()


def step(cap, collective_id, tbl, pairs, adam_v, gram_left, gram_right, root_left, root_right):
    tile = (ROWS, COLS)
    bf, f32 = jnp.bfloat16, jnp.float32
    vm = pltpu.VMEM
    dma = pltpu.SemaphoreType.DMA
    scratch = (
        [vm((BLOCKS,) + tile, bf)] * PARTS
        + [vm((NZ, cap) + tile, bf)] * PARTS
        + [vm((NZ, cap) + tile, bf)] * PARTS
        + [vm((NX, SLOTS, ROWS, ORDER), bf)] * NZ
        + [
            vm((PARTS, BLOCKS) + tile, bf),
            vm((PARTS, NY - 1, BLOCKS) + tile, bf),
            vm((PARTS, BLOCKS) + tile, f32),
            vm((PARTS, NX, SLOTS, NZ) + tile, bf),
            vm((PARTS, NX, SLOTS, NZ) + tile, bf),
            vm((SLOTS, ORDER, ORDER), bf),
            vm((SLOTS, ORDER, ORDER), f32),
            vm((NX, SLOTS, NZ, ROWS, ORDER), bf),
            vm((NZ, cap, ROWS, ORDER), bf),
            vm((NZ, cap, ROWS, ORDER), bf),
            vm((BLOCKS, ROWS, ORDER), f32),
            vm((SLOTS, ORDER, ORDER), f32),
            vm((SLOTS, ORDER, ORDER), f32),
            vm((SLOTS, ORDER, ORDER), bf),
            vm((SLOTS, ORDER, ORDER), bf),
            vm((BLOCKS, COLS), f32),
            vm((NZ - 1, BLOCKS, COLS), f32),
            vm((BLOCKS, COLS), f32),
            vm((NX - 1, BLOCKS, COLS), f32),
            pltpu.SMEM((8, 128), jnp.int32),
            dma((6,)), dma((PARTS,)),
            dma((PARTS * 3,)), dma((PARTS * 3,)),
            dma((PARTS * 7,)), dma((PARTS * 7,)),
            dma((PARTS * 3,)), dma((PARTS * 3,)),
            dma((NZ * 3,)), dma((NZ * 3,)),
            dma((NZ - 1,)), dma((NZ - 1,)),
            dma((10,)), dma((10,)), dma,
        ]
    )
    hbm = pl.BlockSpec(memory_space=pl.ANY)
    return pl.pallas_call(
        functools.partial(step_kernel, cap),
        out_shape=(
            pltpu.VMEM((1, BLOCKS, ROWS, ORDER), bf),
            pltpu.VMEM(gram_left.shape, f32),
            jax.ShapeDtypeStruct(gram_right.shape, f32),
        ),
        in_specs=[hbm] * 7,
        out_specs=(pl.BlockSpec(memory_space=pltpu.VMEM), pl.BlockSpec(memory_space=pltpu.VMEM), hbm),
        scratch_shapes=scratch,
        compiler_params=pltpu.CompilerParams(
            collective_id=collective_id, has_side_effects=True, vmem_limit_bytes=32 << 20
        ),
        name=f"step_{cap}",
    )(tbl, pairs, adam_v, gram_left, gram_right, root_left, root_right)


def place_kernel(upd, gl, gr, upd_out, gl_out, gr_out, held, in_sem, out_sem):
    rows = ORDER // CHUNKS
    pieces = [(s, pl.ds(r * rows, rows)) for s in range(SLOTS) for r in range(CHUNKS)]
    loads = []
    for i, (s, r) in enumerate(pieces):
        copy = pltpu.make_async_copy(gr.at[0, 0, s, r], held.at[s, r], in_sem.at[i])
        copy.start()
        loads.append(copy)
    stores = [pltpu.make_async_copy(upd, upd_out, out_sem.at[0])]
    for i, (s, r) in enumerate(pieces):
        stores.append(pltpu.make_async_copy(gl.at[0, 0, s, r], gl_out.at[0, 0, s, r], out_sem.at[1 + i]))
    for copy in stores:
        copy.start()
    for i, (s, r) in enumerate(pieces):
        loads[i].wait()
        copy = pltpu.make_async_copy(held.at[s, r], gr_out.at[0, 0, s, r], out_sem.at[1 + len(pieces) + i])
        copy.start()
        stores.append(copy)
    for copy in stores:
        copy.wait()


def place(upd, gl, gr):
    hbm = pl.BlockSpec(memory_space=pl.ANY)
    vmem = pl.BlockSpec(memory_space=pltpu.VMEM)
    return pl.pallas_call(
        place_kernel,
        out_shape=tuple(jax.ShapeDtypeStruct(a.shape, a.dtype) for a in (upd, gl, gr)),
        in_specs=[hbm] * 3,
        out_specs=(hbm,) * 3,
        scratch_shapes=[
            pltpu.VMEM((SLOTS, ORDER, ORDER), jnp.float32),
            pltpu.SemaphoreType.DMA((SLOTS * CHUNKS,)),
            pltpu.SemaphoreType.DMA((SLOTS * CHUNKS * 2 + 1,)),
        ],
        compiler_params=pltpu.CompilerParams(vmem_limit_bytes=8 << 20),
        name="place",
    )(upd, gl, gr)


def per_device(grad_part, adam_v, owner_of, gram_left, gram_right, root_left, root_right):
    pairs, table, which = pair_sum(grad_part, owner_of.reshape(BLOCKS))
    operands = (table, pairs, adam_v, gram_left, gram_right, root_left, root_right)
    branches = [functools.partial(step, cap, i + 1) for i, cap in enumerate(CAPS)]
    return place(*lax.switch(which[0], branches, *operands))


def solution(mesh):
    placed = (
        P("grp", None, None, "fsdp", None),
        P("grp", None, "fsdp", None),
        P("grp", None, None),
        P("grp", "fsdp", None, None, None),
        P("grp", "fsdp", None, None, None),
        P("grp", "fsdp", None, None, None),
        P("grp", "fsdp", None, None, None),
    )
    return jax.shard_map(
        per_device,
        mesh=mesh,
        in_specs=placed,
        out_specs=(
            P("grp", None, "fsdp", None),
            P("grp", "fsdp", None, None, None),
            P("grp", "fsdp", None, None, None),
        ),
        check_vma=False,
    )
```

```python
import functools

import jax
import jax.numpy as jnp
from jax import lax
from jax.experimental import pallas as pl
from jax.experimental.pallas import tpu as pltpu
from jax.sharding import PartitionSpec as P

BETA2 = 0.9
EPS_ADAM = 1e-08
EPS_NORM = 1e-06
MESH = pl.DeviceIdType.MESH

NX, NY, NZ = 4, 4, 8
BLOCKS, ROWS, ORDER, SLOTS = 16, 16, 512, 2
PARTS = 4
COLS = ORDER // PARTS
CAPS = (4, 5, 6, 8)
CHUNKS = 2
BACK_ORDER = (4, 3, 5, 2, 6, 1, 7, 0)

T_LIST, T_PLACE, T_OWNED, T_PLANE, T_RANK, T_MINE, T_HELD = 0, 64, 72, 80, 96, 112, 114


def position():
    g = lax.axis_index("grp")
    f = lax.axis_index("fsdp")
    return g, f, g // 2, g % 2, f // NZ, f % NZ


def remote(src, dst, send, recv, device):
    return pltpu.make_async_remote_copy(
        src_ref=src, dst_ref=dst, send_sem=send, recv_sem=recv,
        device_id=device, device_id_type=MESH,
    )


def block_places(owner_ref):
    shape = (BLOCKS, 128)
    row = lax.broadcasted_iota(jnp.int32, shape, 0)
    lane = lax.broadcasted_iota(jnp.int32, shape, 1)
    down = jnp.zeros(shape, jnp.int32)
    across = jnp.zeros(shape, jnp.int32)
    for j in range(BLOCKS):
        down = jnp.where(row == j, owner_ref[j], down)
        across = jnp.where(lane == j, owner_ref[j], across)
    count = lambda same: jnp.sum(jnp.where(same & (lane < row), 1.0, 0.0), axis=1, keepdims=True)
    slot = count(down == across).astype(jnp.int32)
    ranks = count(down % NZ == across % NZ)
    return down, slot, ranks.astype(jnp.int32), jnp.max(ranks, keepdims=True) + 1.0


def index_table(down, slot, rank, me, z):
    shape = (BLOCKS, 128)
    row = lax.broadcasted_iota(jnp.int32, shape, 0)
    lane = lax.broadcasted_iota(jnp.int32, shape, 1)
    plane, line = down % NZ, down // NZ
    here = plane == z
    mine = down == me
    whole = jnp.zeros(shape, jnp.int32)
    for first, size, cond, value in (
        (T_LIST, 64, lambda e: (plane == e // 8) & (rank == e % 8), row),
        (T_PLACE, 8, lambda e: here & (line == e // SLOTS) & (slot == e % SLOTS), rank),
        (T_OWNED, 8, lambda e: here & (rank == e), line * SLOTS + slot),
        (T_PLANE, 16, lambda e: row == e, plane),
        (T_RANK, 16, lambda e: row == e, rank),
        (T_MINE, 2, lambda e: mine & (slot == e), row),
        (T_HELD, 2, lambda e: mine & (slot == e), 1),
    ):
        entry = lane - first
        whole += jnp.where((entry >= 0) & (entry < size) & cond(entry), value, 0)
    return jnp.sum(whole.astype(jnp.float32), axis=0, keepdims=True).astype(jnp.int32)


def pair_kernel(parts_ref, owner_hbm, out_ref, first_ref, tbl_ref, which_hbm,
                owner_ref, which_ref, small_sem, own, other, pair, yrecv, load, loads, own_sem, send, recv, lsend, lrecv, ysend, yrecv_sem):
    g, f, y, c, x, z = position()
    owner_copy = pltpu.make_async_copy(owner_hbm, owner_ref, small_sem.at[0])
    owner_copy.start()
    barrier = pltpu.get_barrier_semaphore()
    for d in range(1, 8):
        pl.semaphore_signal(barrier, inc=1, device_id=((g + d) % 8, f), device_id_type=MESH)
    own_copies = []
    for p in range(PARTS):
        cols = pl.ds(p * COLS, COLS)
        copy = pltpu.make_async_copy(parts_ref.at[:, c, :, :, cols], own.at[p], own_sem.at[p])
        copy.start()
        own_copies.append(copy)
    owner_copy.wait()
    down, slot, rank, most = block_places(owner_ref)
    load[...] = jnp.broadcast_to(most, (8, 128))
    pl.semaphore_wait(barrier, 7)
    copies = []
    for p in range(PARTS):
        cols = pl.ds(p * COLS, COLS)
        copy = remote(parts_ref.at[:, 1 - c, :, :, cols], other.at[p], send.at[p], recv.at[p], (y * 2 + 1 - c, f))
        copy.start()
        copies.append(copy)
    load_copies = []
    for d in range(1, 8):
        copy = remote(load, loads.at[d], lsend.at[d], lrecv.at[d], ((g + d) % 8, f))
        copy.start()
        load_copies.append(copy)
    own_copies[0].wait()
    copies[0].wait_recv()
    pair[...] = own[0] + other[0]
    y_copies = []
    for d in range(1, NY):
        to = (y + d) % NY
        copy = remote(pair.at[to], yrecv.at[d - 1], ysend.at[d - 1], yrecv_sem.at[d - 1], (to * 2 + c, f))
        copy.start()
        y_copies.append(copy)
    tbl_ref[...] = jnp.broadcast_to(index_table(down, slot, rank, f, z), (8, 128))
    for p in range(1, PARTS):
        own_copies[p].wait()
        copies[p].wait_recv()
        out_ref[p - 1] = own[p] + other[p]
    most = load[...]
    for d in range(1, 8):
        load_copies[d - 1].wait_recv()
        most = jnp.maximum(most, loads[d])
    most = jnp.max(most)
    which_ref[0] = sum((most > cap).astype(jnp.int32) for cap in CAPS[:-1])
    which_copy = pltpu.make_async_copy(which_ref, which_hbm, small_sem.at[1])
    which_copy.start()
    for copy in load_copies + copies:
        copy.wait_send()
    total = pair[y].astype(jnp.float32)
    for d in range(NY - 1):
        y_copies[d].wait_recv()
        total = total + yrecv[d].astype(jnp.float32)
    first_ref[...] = total
    which_copy.wait()
    for copy in y_copies:
        copy.wait_send()


def pair_sum(grad_part, owner_ids):
    part = (BLOCKS, ROWS, COLS)
    vmem = pl.BlockSpec(memory_space=pltpu.VMEM)
    hbm = pl.BlockSpec(memory_space=pl.ANY)
    return pl.pallas_call(
        pair_kernel,
        out_shape=(
            jax.ShapeDtypeStruct((PARTS - 1, NY) + part, jnp.bfloat16),
            jax.ShapeDtypeStruct(part, jnp.float32),
            jax.ShapeDtypeStruct((8, 128), jnp.int32),
            jax.ShapeDtypeStruct((1,), jnp.int32),
        ),
        in_specs=[hbm, hbm],
        out_specs=(vmem, vmem, vmem, hbm),
        scratch_shapes=[
            pltpu.SMEM((BLOCKS,), jnp.int32),
            pltpu.SMEM((1,), jnp.int32),
            pltpu.SemaphoreType.DMA((2,)),
            pltpu.VMEM((PARTS, NY) + part, jnp.bfloat16),
            pltpu.VMEM((PARTS, NY) + part, jnp.bfloat16),
            pltpu.VMEM((NY,) + part, jnp.bfloat16),
            pltpu.VMEM((NY - 1,) + part, jnp.bfloat16),
            pltpu.VMEM((8, 128), jnp.float32),
            pltpu.VMEM((8, 8, 128), jnp.float32),
            pltpu.SemaphoreType.DMA((PARTS,)),
            pltpu.SemaphoreType.DMA((PARTS,)),
            pltpu.SemaphoreType.DMA((PARTS,)),
            pltpu.SemaphoreType.DMA((8,)),
            pltpu.SemaphoreType.DMA((8,)),
            pltpu.SemaphoreType.DMA((NY - 1,)),
            pltpu.SemaphoreType.DMA((NY - 1,)),
        ],
        compiler_params=pltpu.CompilerParams(
            collective_id=0, has_side_effects=True, vmem_limit_bytes=60 << 20
        ),
        name="pair_sum",
    )(grad_part, owner_ids)


def step_kernel(cap, tbl_hbm, pairs, first, adam_hbm, gl_hbm, gr_hbm, rl_hbm, rr_hbm,
                upd, gl_out, gr_out, *scratch):
    scratch = list(scratch)
    take = lambda n: [scratch.pop(0) for _ in range(n)]
    gbf, zsend, zrecv = (take(PARTS) for _ in range(3))
    xret = take(NZ)
    (yown, yrecv, gsum, xsend, xrecv, gmat, dirb, xback, zback, zret, adam, gl, gr, rl, rr,
     gpart, gzrecv, gzsum, gxrecv, tbls,
     lsem, ysem, ysend_sem, yrecv_sem, zsend_sem, zrecv_sem, xsend_sem, xrecv_sem,
     bxsend_sem, bxrecv_sem, bzsend_sem, bzrecv_sem, gsend_sem, grecv_sem, osem) = scratch
    g, f, y, c, x, z = position()
    at_y = lambda i: (i * 2 + c, f)
    at_z = lambda i: (g, x * NZ + i)
    at_x = lambda i: (g, i * NZ + z)
    plus = lambda a, d, n: (a + d) % n
    sends = []

    def start(copy):
        copy.start()
        sends.append(copy)
        return copy

    own_copies = []
    copy = pltpu.make_async_copy(first, gsum.at[0], ysem.at[0])
    copy.start()
    own_copies.append(copy)
    for p in range(1, PARTS):
        copy = pltpu.make_async_copy(pairs.at[p - 1, y], yown.at[p - 1], ysem.at[p])
        copy.start()
        own_copies.append(copy)
    big = []
    for i, (src, dst) in enumerate(((adam_hbm.at[0], adam), (rl_hbm.at[0, 0], rl), (rr_hbm.at[0, 0], rr),
                                    (gl_hbm.at[0, 0], gl), (gr_hbm.at[0, 0], gr), (tbl_hbm, tbls))):
        copy = pltpu.make_async_copy(src, dst, lsem.at[i])
        copy.start()
        big.append(copy)

    barrier = pltpu.get_barrier_semaphore()
    partners = (
        [at_y(plus(y, d, NY)) for d in range(1, NY)]
        + [at_z(plus(z, d, NZ)) for d in range(1, NZ)]
        + [at_x(plus(x, d, NX)) for d in range(1, NX)]
    )
    for partner in partners:
        pl.semaphore_signal(barrier, inc=1, device_id=partner, device_id_type=MESH)
    pl.semaphore_wait(barrier, len(partners))

    y_copies = [[] for _ in range(PARTS)]

    def exchange(p):
        for d in range(1, NY):
            to = plus(y, d, NY)
            n = (p - 1) * 3 + d - 1
            y_copies[p].append(start(remote(
                pairs.at[p - 1, to], yrecv.at[p - 1, d - 1], ysend_sem.at[n], yrecv_sem.at[n], at_y(to))))

    z_copies = [[] for _ in range(PARTS)]
    x_copies = [[] for _ in range(PARTS + 1)]

    def tbl(i):
        return tbls[0, i]

    def reduce_part(p):
        own_copies[p].wait()
        for copy in y_copies[p]:
            copy.wait_recv()
        if p == 0:
            gbf[p][...] = gsum[p].astype(jnp.bfloat16)
        else:
            total = yown[p - 1].astype(jnp.float32)
            for d in range(NY - 1):
                total = total + yrecv[p - 1, d].astype(jnp.float32)
            gsum[p] = total
            gbf[p][...] = total.astype(jnp.bfloat16)

        @pl.loop(0, NZ)
        def _(i):
            for k in range(cap):
                zsend[p][i, k] = gbf[p][tbl(T_LIST + i * 8 + k)]

        for d in range(1, NZ):
            to = plus(z, d, NZ)
            n = p * 7 + d - 1
            z_copies[p].append(start(remote(
                zsend[p].at[to], zrecv[p].at[z], zsend_sem.at[n], zrecv_sem.at[n], at_z(to))))
        zrecv[p][z] = zsend[p][z]

    def pass_on(p):
        for copy in z_copies[p]:
            copy.wait_recv()

        for i in range(NX * SLOTS):
            k = tbl(T_PLACE + i)
            for r in range(NZ):
                xsend[p, i // SLOTS, i % SLOTS, r] = zrecv[p][r, k]

        if p < PARTS - 1:
            for d in range(1, NX):
                to = plus(x, d, NX)
                n = p * 3 + d - 1
                x_copies[p].append(start(remote(
                    xsend.at[p, to], xrecv.at[p, x], xsend_sem.at[n], xrecv_sem.at[n], at_x(to))))
        else:
            for s in range(SLOTS):
                for d in range(1, NX):
                    to = plus(x, d, NX)
                    n = (p + s) * 3 + d - 1
                    x_copies[p + s].append(start(remote(
                        xsend.at[p, to, s], xrecv.at[p, x, s], xsend_sem.at[n], xrecv_sem.at[n], at_x(to))))
        xrecv[p, x] = xsend[p, x]

    def apply_roots(p, s):
        block = xrecv[p, :, s].reshape(ORDER, COLS)
        gmat[s, :, p * COLS:(p + 1) * COLS] = block
        left = jnp.dot(rl[s], block, preferred_element_type=jnp.float32).astype(jnp.bfloat16)
        term = jnp.dot(left, rr[s, p * COLS:(p + 1) * COLS, :], preferred_element_type=jnp.float32)
        term = term.reshape(NX, NZ, ROWS, ORDER)
        if p == 0:
            dirb[s] = term
        else:
            dirb[s] += term

    def apply_both(p):
        for copy in x_copies[p]:
            copy.wait_recv()
        pl.loop(0, SLOTS)(lambda s: apply_roots(p, s))

    graft_z = []
    graft_x = []

    def graft_first():
        big[0].wait()
        part = jnp.zeros((BLOCKS, COLS), jnp.float32)
        for p in range(PARTS):
            total = gsum[p]
            second = BETA2 * adam[:, :, p * COLS:(p + 1) * COLS] + (1.0 - BETA2) * total * total
            ratio = total / (jnp.sqrt(second) + EPS_ADAM)
            part = part + jnp.sum(ratio * ratio, axis=1)
        gpart[...] = part
        for d in range(1, NZ):
            graft_z.append(start(remote(
                gpart, gzrecv.at[d - 1], gsend_sem.at[d - 1], grecv_sem.at[d - 1], at_z(plus(z, d, NZ)))))

    def graft_second():
        total = gpart[...]
        for d in range(NZ - 1):
            graft_z[d].wait_recv()
            total = total + gzrecv[d]
        gzsum[...] = total
        for d in range(1, NX):
            n = 6 + d
            graft_x.append(start(remote(
                gzsum, gxrecv.at[d - 1], gsend_sem.at[n], grecv_sem.at[n], at_x(plus(x, d, NX)))))

    exchange(1)
    big[5].wait()
    reduce_part(0)
    for p in range(2, PARTS):
        exchange(p)
    reduce_part(1)
    pass_on(0)
    reduce_part(2)
    pass_on(1)
    reduce_part(3)
    graft_first()
    big[1].wait()
    big[2].wait()
    apply_both(0)
    pass_on(2)
    graft_second()
    apply_both(1)
    pass_on(3)
    apply_both(2)
    graft = gzsum[...]
    for d in range(NX - 1):
        graft_x[d].wait_recv()
        graft = graft + gxrecv[d]
    block_ids = lax.broadcasted_iota(jnp.int32, (BLOCKS, COLS), 0)
    graft_norms = []
    for s in range(SLOTS):
        graft_norms.append(jnp.sqrt(jnp.sum(jnp.where(block_ids == tbl(T_MINE + s), graft, 0.0), keepdims=True)))
    scales = []
    for s in range(SLOTS):
        for copy in x_copies[PARTS - 1 + s]:
            copy.wait_recv()
        apply_roots(PARTS - 1, s)
        whole = dirb[s]
        norm = jnp.sqrt(jnp.sum((whole * whole).reshape(ORDER, ORDER), keepdims=True))
        scales.append(-(graft_norms[s] / (norm + EPS_NORM)))
    forward = list(sends)
    bx_copies = [[] for _ in range(NZ)]
    bz_copies = []
    for d in BACK_ORDER:
        plane = plus(z, d, NZ)
        for s in range(SLOTS):
            xback[d, :, s] = (dirb[s, :, plane] * scales[s]).astype(jnp.bfloat16)
        for e in range(1, NX):
            to = plus(x, e, NX)
            n = d * 3 + e - 1
            bx_copies[d].append(start(remote(
                xback.at[d, to], xret[d].at[x], bxsend_sem.at[n], bxrecv_sem.at[n], at_x(to))))
        xret[d][x] = xback[d, x]

    big[3].wait()
    big[4].wait()

    @pl.loop(0, SLOTS)
    def _(s):
        held = tbl(T_HELD + s) > 0
        block = gmat[s]
        outer = lax.dot_general(block, block, (((1,), (1,)), ((), ())), preferred_element_type=jnp.float32)
        gl_out[0, 0, s] = gl[s] + jnp.where(held, outer, 0.0)
        outer = lax.dot_general(block, block, (((0,), (0,)), ((), ())), preferred_element_type=jnp.float32)
        gr[s] = gr[s] + jnp.where(held, outer, 0.0)

    out_copy = pltpu.make_async_copy(gr, gr_out.at[0, 0], osem)
    out_copy.start()

    for copy in forward:
        copy.wait_send()
    for d in BACK_ORDER:
        for copy in bx_copies[d]:
            copy.wait_recv()
        land = zback if d else zret
        for k in range(cap):
            e = tbl(T_OWNED + k)
            land[d, k] = xret[d][e // SLOTS, e % SLOTS]
        if d:
            bz_copies.append(start(remote(
                zback.at[d], zret.at[d], bzsend_sem.at[d - 1], bzrecv_sem.at[d - 1], at_z(plus(z, d, NZ)))))
    out_copy.wait()
    for copies in bx_copies:
        for copy in copies:
            copy.wait_send()
    for copy in bz_copies:
        copy.wait()
    for j in range(BLOCKS):
        away = (z + NZ - tbl(T_PLANE + j)) % NZ
        upd[0, j] = zret[away, tbl(T_RANK + j)]


def step(cap, collective_id, tbl, pairs, first, adam_v, gram_left, gram_right, root_left, root_right):
    tile = (ROWS, COLS)
    bf, f32 = jnp.bfloat16, jnp.float32
    vm = pltpu.VMEM
    dma = pltpu.SemaphoreType.DMA
    scratch = (
        [vm((BLOCKS,) + tile, bf)] * PARTS
        + [vm((NZ, cap) + tile, bf)] * PARTS
        + [vm((NZ, cap) + tile, bf)] * PARTS
        + [vm((NX, SLOTS, ROWS, ORDER), bf)] * NZ
        + [
            vm((PARTS - 1, BLOCKS) + tile, bf),
            vm((PARTS - 1, NY - 1, BLOCKS) + tile, bf),
            vm((PARTS, BLOCKS) + tile, f32),
            vm((PARTS, NX, SLOTS, NZ) + tile, bf),
            vm((PARTS, NX, SLOTS, NZ) + tile, bf),
            vm((SLOTS, ORDER, ORDER), bf),
            vm((SLOTS, NX, NZ, ROWS, ORDER), f32),
            vm((NZ, NX, SLOTS, ROWS, ORDER), bf),
            vm((NZ, cap, ROWS, ORDER), bf),
            vm((NZ, cap, ROWS, ORDER), bf),
            vm((BLOCKS, ROWS, ORDER), f32),
            vm((SLOTS, ORDER, ORDER), f32),
            vm((SLOTS, ORDER, ORDER), f32),
            vm((SLOTS, ORDER, ORDER), bf),
            vm((SLOTS, ORDER, ORDER), bf),
            vm((BLOCKS, COLS), f32),
            vm((NZ - 1, BLOCKS, COLS), f32),
            vm((BLOCKS, COLS), f32),
            vm((NX - 1, BLOCKS, COLS), f32),
            pltpu.SMEM((8, 128), jnp.int32),
            dma((6,)), dma((PARTS,)),
            dma((PARTS * 3 - 3,)), dma((PARTS * 3 - 3,)),
            dma((PARTS * 7,)), dma((PARTS * 7,)),
            dma((PARTS * 3 + 3,)), dma((PARTS * 3 + 3,)),
            dma((NZ * 3,)), dma((NZ * 3,)),
            dma((NZ - 1,)), dma((NZ - 1,)),
            dma((10,)), dma((10,)), dma,
        ]
    )
    hbm = pl.BlockSpec(memory_space=pl.ANY)
    return pl.pallas_call(
        functools.partial(step_kernel, cap),
        out_shape=(
            pltpu.VMEM((1, BLOCKS, ROWS, ORDER), bf),
            pltpu.VMEM(gram_left.shape, f32),
            jax.ShapeDtypeStruct(gram_right.shape, f32),
        ),
        in_specs=[hbm] * 8,
        out_specs=(pl.BlockSpec(memory_space=pltpu.VMEM), pl.BlockSpec(memory_space=pltpu.VMEM), hbm),
        scratch_shapes=scratch,
        compiler_params=pltpu.CompilerParams(
            collective_id=collective_id, has_side_effects=True, vmem_limit_bytes=32 << 20
        ),
        name=f"step_{cap}",
    )(tbl, pairs, first, adam_v, gram_left, gram_right, root_left, root_right)


def place_kernel(upd, gl, gr, upd_out, gl_out, gr_out, held, in_sem, out_sem):
    rows = ORDER // CHUNKS
    pieces = [(s, pl.ds(r * rows, rows)) for s in range(SLOTS) for r in range(CHUNKS)]
    loads = []
    for i, (s, r) in enumerate(pieces):
        copy = pltpu.make_async_copy(gr.at[0, 0, s, r], held.at[s, r], in_sem.at[i])
        copy.start()
        loads.append(copy)
    stores = [pltpu.make_async_copy(upd, upd_out, out_sem.at[0])]
    for i, (s, r) in enumerate(pieces):
        stores.append(pltpu.make_async_copy(gl.at[0, 0, s, r], gl_out.at[0, 0, s, r], out_sem.at[1 + i]))
    for copy in stores:
        copy.start()
    for i, (s, r) in enumerate(pieces):
        loads[i].wait()
        copy = pltpu.make_async_copy(held.at[s, r], gr_out.at[0, 0, s, r], out_sem.at[1 + len(pieces) + i])
        copy.start()
        stores.append(copy)
    for copy in stores:
        copy.wait()


def place(upd, gl, gr):
    hbm = pl.BlockSpec(memory_space=pl.ANY)
    vmem = pl.BlockSpec(memory_space=pltpu.VMEM)
    return pl.pallas_call(
        place_kernel,
        out_shape=tuple(jax.ShapeDtypeStruct(a.shape, a.dtype) for a in (upd, gl, gr)),
        in_specs=[hbm] * 3,
        out_specs=(hbm,) * 3,
        scratch_shapes=[
            pltpu.VMEM((SLOTS, ORDER, ORDER), jnp.float32),
            pltpu.SemaphoreType.DMA((SLOTS * CHUNKS,)),
            pltpu.SemaphoreType.DMA((SLOTS * CHUNKS * 2 + 1,)),
        ],
        compiler_params=pltpu.CompilerParams(vmem_limit_bytes=8 << 20),
        name="place",
    )(upd, gl, gr)


def per_device(grad_part, adam_v, owner_of, gram_left, gram_right, root_left, root_right):
    by_core = grad_part.reshape((NY, 2) + grad_part.shape[2:])
    pairs, first, table, which = pair_sum(by_core, owner_of.reshape(BLOCKS))
    operands = (table, pairs, first, adam_v, gram_left, gram_right, root_left, root_right)
    branches = [functools.partial(step, cap, i + 1) for i, cap in enumerate(CAPS)]
    return place(*lax.switch(which[0], branches, *operands))


def solution(mesh):
    placed = (
        P("grp", None, None, "fsdp", None),
        P("grp", None, "fsdp", None),
        P("grp", None, None),
        P("grp", "fsdp", None, None, None),
        P("grp", "fsdp", None, None, None),
        P("grp", "fsdp", None, None, None),
        P("grp", "fsdp", None, None, None),
    )
    return jax.shard_map(
        per_device,
        mesh=mesh,
        in_specs=placed,
        out_specs=(
            P("grp", None, "fsdp", None),
            P("grp", "fsdp", None, None, None),
            P("grp", "fsdp", None, None, None),
        ),
        check_vma=False,
    )
```

```python
import functools

import jax
import jax.numpy as jnp
from jax import lax
from jax.experimental import pallas as pl
from jax.experimental.pallas import tpu as pltpu
from jax.sharding import PartitionSpec as P

BETA2 = 0.9
EPS_ADAM = 1e-08
EPS_NORM = 1e-06
MESH = pl.DeviceIdType.MESH

NX, NY, NZ = 4, 4, 8
BLOCKS, ROWS, ORDER, SLOTS = 16, 16, 512, 2
PARTS = 4
COLS = ORDER // PARTS
CAPS = (4, 5, 6, 8)
CHUNKS = 2
BACK_ORDER = (4, 3, 5, 2, 6, 1, 7, 0)

T_LIST, T_PLACE, T_OWNED, T_PLANE, T_RANK, T_MINE, T_HELD = 0, 64, 72, 80, 96, 112, 114


def position():
    g = lax.axis_index("grp")
    f = lax.axis_index("fsdp")
    return g, f, g // 2, g % 2, f // NZ, f % NZ


def remote(src, dst, send, recv, device):
    return pltpu.make_async_remote_copy(
        src_ref=src, dst_ref=dst, send_sem=send, recv_sem=recv,
        device_id=device, device_id_type=MESH,
    )


def block_places(owner_ref):
    shape = (BLOCKS, 128)
    row = lax.broadcasted_iota(jnp.int32, shape, 0)
    lane = lax.broadcasted_iota(jnp.int32, shape, 1)
    down = jnp.zeros(shape, jnp.int32)
    across = jnp.zeros(shape, jnp.int32)
    for j in range(BLOCKS):
        down = jnp.where(row == j, owner_ref[j], down)
        across = jnp.where(lane == j, owner_ref[j], across)
    count = lambda same: jnp.sum(jnp.where(same & (lane < row), 1.0, 0.0), axis=1, keepdims=True)
    slot = count(down == across).astype(jnp.int32)
    ranks = count(down % NZ == across % NZ)
    return down, slot, ranks.astype(jnp.int32), jnp.max(ranks, keepdims=True) + 1.0


def index_table(down, slot, rank, me, z):
    shape = (BLOCKS, 128)
    row = lax.broadcasted_iota(jnp.int32, shape, 0)
    lane = lax.broadcasted_iota(jnp.int32, shape, 1)
    plane, line = down % NZ, down // NZ
    here = plane == z
    mine = down == me
    whole = jnp.zeros(shape, jnp.int32)
    for first, size, cond, value in (
        (T_LIST, 64, lambda e: (plane == e // 8) & (rank == e % 8), row),
        (T_PLACE, 8, lambda e: here & (line == e // SLOTS) & (slot == e % SLOTS), rank),
        (T_OWNED, 8, lambda e: here & (rank == e), line * SLOTS + slot),
        (T_PLANE, 16, lambda e: row == e, plane),
        (T_RANK, 16, lambda e: row == e, rank),
        (T_MINE, 2, lambda e: mine & (slot == e), row),
        (T_HELD, 2, lambda e: mine & (slot == e), 1),
    ):
        entry = lane - first
        whole += jnp.where((entry >= 0) & (entry < size) & cond(entry), value, 0)
    return jnp.sum(whole.astype(jnp.float32), axis=0, keepdims=True).astype(jnp.int32)


def pair_kernel(parts_ref, owner_hbm, out_ref, first_ref, tbl_ref, which_hbm,
                owner_ref, which_ref, small_sem, own, other, pair, yrecv, load, loads, own_sem, send, recv, lsend, lrecv, ysend, yrecv_sem):
    g, f, y, c, x, z = position()
    owner_copy = pltpu.make_async_copy(owner_hbm, owner_ref, small_sem.at[0])
    owner_copy.start()
    barrier = pltpu.get_barrier_semaphore()
    for d in range(1, 8):
        pl.semaphore_signal(barrier, inc=1, device_id=((g + d) % 8, f), device_id_type=MESH)
    own_copies = []
    for p in range(PARTS):
        cols = pl.ds(p * COLS, COLS)
        copy = pltpu.make_async_copy(parts_ref.at[:, c, :, :, cols], own.at[p], own_sem.at[p])
        copy.start()
        own_copies.append(copy)
    owner_copy.wait()
    down, slot, rank, most = block_places(owner_ref)
    load[...] = jnp.broadcast_to(most, (8, 128))
    pl.semaphore_wait(barrier, 7)
    copies = []
    for p in range(PARTS):
        cols = pl.ds(p * COLS, COLS)
        copy = remote(parts_ref.at[:, 1 - c, :, :, cols], other.at[p], send.at[p], recv.at[p], (y * 2 + 1 - c, f))
        copy.start()
        copies.append(copy)
    load_copies = []
    for d in range(1, 8):
        copy = remote(load, loads.at[d], lsend.at[d], lrecv.at[d], ((g + d) % 8, f))
        copy.start()
        load_copies.append(copy)
    own_copies[0].wait()
    copies[0].wait_recv()
    pair[...] = own[0] + other[0]
    y_copies = []
    for d in range(1, NY):
        to = (y + d) % NY
        copy = remote(pair.at[to], yrecv.at[d - 1], ysend.at[d - 1], yrecv_sem.at[d - 1], (to * 2 + c, f))
        copy.start()
        y_copies.append(copy)
    tbl_ref[...] = jnp.broadcast_to(index_table(down, slot, rank, f, z), (8, 128))
    for p in range(1, PARTS):
        own_copies[p].wait()
        copies[p].wait_recv()
        out_ref[p - 1] = own[p] + other[p]
    most = load[...]
    for d in range(1, 8):
        load_copies[d - 1].wait_recv()
        most = jnp.maximum(most, loads[d])
    most = jnp.max(most)
    which_ref[0] = sum((most > cap).astype(jnp.int32) for cap in CAPS[:-1])
    which_copy = pltpu.make_async_copy(which_ref, which_hbm, small_sem.at[1])
    which_copy.start()
    for copy in load_copies + copies:
        copy.wait_send()
    total = pair[y].astype(jnp.float32)
    for d in range(NY - 1):
        y_copies[d].wait_recv()
        total = total + yrecv[d].astype(jnp.float32)
    first_ref[...] = total
    which_copy.wait()
    for copy in y_copies:
        copy.wait_send()


def pair_sum(grad_part, owner_ids):
    part = (BLOCKS, ROWS, COLS)
    vmem = pl.BlockSpec(memory_space=pltpu.VMEM)
    hbm = pl.BlockSpec(memory_space=pl.ANY)
    return pl.pallas_call(
        pair_kernel,
        out_shape=(
            jax.ShapeDtypeStruct((PARTS - 1, NY) + part, jnp.bfloat16),
            jax.ShapeDtypeStruct(part, jnp.float32),
            jax.ShapeDtypeStruct((8, 128), jnp.int32),
            jax.ShapeDtypeStruct((1,), jnp.int32),
        ),
        in_specs=[hbm, hbm],
        out_specs=(vmem, vmem, vmem, hbm),
        scratch_shapes=[
            pltpu.SMEM((BLOCKS,), jnp.int32),
            pltpu.SMEM((1,), jnp.int32),
            pltpu.SemaphoreType.DMA((2,)),
            pltpu.VMEM((PARTS, NY) + part, jnp.bfloat16),
            pltpu.VMEM((PARTS, NY) + part, jnp.bfloat16),
            pltpu.VMEM((NY,) + part, jnp.bfloat16),
            pltpu.VMEM((NY - 1,) + part, jnp.bfloat16),
            pltpu.VMEM((8, 128), jnp.float32),
            pltpu.VMEM((8, 8, 128), jnp.float32),
            pltpu.SemaphoreType.DMA((PARTS,)),
            pltpu.SemaphoreType.DMA((PARTS,)),
            pltpu.SemaphoreType.DMA((PARTS,)),
            pltpu.SemaphoreType.DMA((8,)),
            pltpu.SemaphoreType.DMA((8,)),
            pltpu.SemaphoreType.DMA((NY - 1,)),
            pltpu.SemaphoreType.DMA((NY - 1,)),
        ],
        compiler_params=pltpu.CompilerParams(
            collective_id=0, has_side_effects=True, vmem_limit_bytes=60 << 20
        ),
        name="pair_sum",
    )(grad_part, owner_ids)


def step_kernel(cap, tbl_hbm, pairs, first, adam_hbm, gl_hbm, gr_hbm, rl_hbm, rr_hbm,
                upd, gl_out, gr_out0, gr_out1, *scratch):
    scratch = list(scratch)
    take = lambda n: [scratch.pop(0) for _ in range(n)]
    gbf, zsend, zrecv = (take(PARTS) for _ in range(3))
    xret = take(NZ)
    (yown, yrecv, gsum, xsend, xrecv, gmat, dirb, xback, zback, zret, adam, gl, gr, rl, rr,
     gpart, gzrecv, gzsum, gxrecv, tbls,
     lsem, ysem, ysend_sem, yrecv_sem, zsend_sem, zrecv_sem, xsend_sem, xrecv_sem,
     bxsend_sem, bxrecv_sem, bzsend_sem, bzrecv_sem, gsend_sem, grecv_sem, osem) = scratch
    g, f, y, c, x, z = position()
    at_y = lambda i: (i * 2 + c, f)
    at_z = lambda i: (g, x * NZ + i)
    at_x = lambda i: (g, i * NZ + z)
    plus = lambda a, d, n: (a + d) % n
    sends = []

    def start(copy):
        copy.start()
        sends.append(copy)
        return copy

    barrier = pltpu.get_barrier_semaphore()
    partners = (
        [at_y(plus(y, d, NY)) for d in range(1, NY)]
        + [at_z(plus(z, d, NZ)) for d in range(1, NZ)]
        + [at_x(plus(x, d, NX)) for d in range(1, NX)]
    )
    for partner in partners:
        pl.semaphore_signal(barrier, inc=1, device_id=partner, device_id_type=MESH)
    own_copies = []
    copy = pltpu.make_async_copy(first, gsum.at[0], ysem.at[0])
    copy.start()
    own_copies.append(copy)
    for p in range(1, PARTS):
        copy = pltpu.make_async_copy(pairs.at[p - 1, y], yown.at[p - 1], ysem.at[p])
        copy.start()
        own_copies.append(copy)
    big = []
    for i, (src, dst) in enumerate(((adam_hbm.at[0], adam), (rl_hbm.at[0, 0], rl), (rr_hbm.at[0, 0], rr),
                                    (gl_hbm.at[0, 0], gl), (gr_hbm.at[0, 0], gr), (tbl_hbm, tbls))):
        copy = pltpu.make_async_copy(src, dst, lsem.at[i])
        if i not in (3, 4):
            copy.start()
        big.append(copy)

    y_copies = [[] for _ in range(PARTS)]

    def exchange(p):
        for d in range(1, NY):
            to = plus(y, d, NY)
            n = (p - 1) * 3 + d - 1
            y_copies[p].append(start(remote(
                pairs.at[p - 1, to], yrecv.at[p - 1, d - 1], ysend_sem.at[n], yrecv_sem.at[n], at_y(to))))

    z_copies = [[] for _ in range(PARTS)]
    x_copies = [[] for _ in range(PARTS + 1)]

    def tbl(i):
        return tbls[0, i]

    def reduce_part(p):
        own_copies[p].wait()
        for copy in y_copies[p]:
            copy.wait_recv()
        if p == 0:
            gbf[p][...] = gsum[p].astype(jnp.bfloat16)
        else:
            total = yown[p - 1].astype(jnp.float32)
            for d in range(NY - 1):
                total = total + yrecv[p - 1, d].astype(jnp.float32)
            gsum[p] = total
            gbf[p][...] = total.astype(jnp.bfloat16)

        @pl.loop(0, NZ)
        def _(i):
            for k in range(cap):
                zsend[p][i, k] = gbf[p][tbl(T_LIST + i * 8 + k)]
        zrecv[p][z] = zsend[p][z]

    def send_part(p):
        for d in range(1, NZ):
            to = plus(z, d, NZ)
            n = p * 7 + d - 1
            z_copies[p].append(start(remote(
                zsend[p].at[to], zrecv[p].at[z], zsend_sem.at[n], zrecv_sem.at[n], at_z(to))))

    def pass_on(p):
        for copy in z_copies[p]:
            copy.wait_recv()

        for i in range(NX * SLOTS):
            k = tbl(T_PLACE + i)
            for r in range(NZ):
                xsend[p, i // SLOTS, i % SLOTS, r] = zrecv[p][r, k]

        if p < PARTS - 1:
            for d in range(1, NX):
                to = plus(x, d, NX)
                n = p * 3 + d - 1
                x_copies[p].append(start(remote(
                    xsend.at[p, to], xrecv.at[p, x], xsend_sem.at[n], xrecv_sem.at[n], at_x(to))))
        else:
            for s in range(SLOTS):
                for d in range(1, NX):
                    to = plus(x, d, NX)
                    n = (p + s) * 3 + d - 1
                    x_copies[p + s].append(start(remote(
                        xsend.at[p, to, s], xrecv.at[p, x, s], xsend_sem.at[n], xrecv_sem.at[n], at_x(to))))
        xrecv[p, x] = xsend[p, x]

    def apply_roots(p, s):
        block = xrecv[p, :, s].reshape(ORDER, COLS)
        gmat[s, :, p * COLS:(p + 1) * COLS] = block
        left = jnp.dot(rl[s], block, preferred_element_type=jnp.float32).astype(jnp.bfloat16)
        term = jnp.dot(left, rr[s, p * COLS:(p + 1) * COLS, :], preferred_element_type=jnp.float32)
        term = term.reshape(NX, NZ, ROWS, ORDER)
        if p == 0:
            dirb[s] = term
        else:
            dirb[s] += term

    def apply_both(p):
        for copy in x_copies[p]:
            copy.wait_recv()
        pl.loop(0, SLOTS)(lambda s: apply_roots(p, s))

    graft_z = []
    graft_x = []

    def graft_first():
        big[0].wait()
        part = jnp.zeros((BLOCKS, COLS), jnp.float32)
        for p in range(PARTS):
            total = gsum[p]
            second = BETA2 * adam[:, :, p * COLS:(p + 1) * COLS] + (1.0 - BETA2) * total * total
            ratio = total / (jnp.sqrt(second) + EPS_ADAM)
            part = part + jnp.sum(ratio * ratio, axis=1)
        gpart[...] = part
        for d in range(1, NZ):
            graft_z.append(start(remote(
                gpart, gzrecv.at[d - 1], gsend_sem.at[d - 1], grecv_sem.at[d - 1], at_z(plus(z, d, NZ)))))

    def graft_second():
        total = gpart[...]
        for d in range(NZ - 1):
            graft_z[d].wait_recv()
            total = total + gzrecv[d]
        gzsum[...] = total
        for d in range(1, NX):
            n = 6 + d
            graft_x.append(start(remote(
                gzsum, gxrecv.at[d - 1], gsend_sem.at[n], grecv_sem.at[n], at_x(plus(x, d, NX)))))

    big[5].wait()
    reduce_part(0)
    pl.semaphore_wait(barrier, len(partners))
    exchange(1)
    send_part(0)
    for p in range(2, PARTS):
        exchange(p)
    reduce_part(1)
    send_part(1)
    pass_on(0)
    reduce_part(2)
    send_part(2)
    pass_on(1)
    reduce_part(3)
    send_part(3)
    big[3].start()
    big[4].start()
    graft_first()
    big[1].wait()
    big[2].wait()
    apply_both(0)
    pass_on(2)
    graft_second()
    apply_both(1)
    pass_on(3)
    apply_both(2)
    graft = gzsum[...]
    for d in range(NX - 1):
        graft_x[d].wait_recv()
        graft = graft + gxrecv[d]
    block_ids = lax.broadcasted_iota(jnp.int32, (BLOCKS, COLS), 0)
    graft_norms = []
    for s in range(SLOTS):
        graft_norms.append(jnp.sqrt(jnp.sum(jnp.where(block_ids == tbl(T_MINE + s), graft, 0.0), keepdims=True)))
    scales = []
    for s in range(SLOTS):
        for copy in x_copies[PARTS - 1 + s]:
            copy.wait_recv()
        apply_roots(PARTS - 1, s)
        whole = dirb[s]
        norm = jnp.sqrt(jnp.sum((whole * whole).reshape(ORDER, ORDER), keepdims=True))
        scales.append(-(graft_norms[s] / (norm + EPS_NORM)))
    forward = list(sends)
    bx_copies = [[] for _ in range(NZ)]
    bz_copies = []
    for d in BACK_ORDER:
        plane = plus(z, d, NZ)
        for s in range(SLOTS):
            xback[d, :, s] = (dirb[s, :, plane] * scales[s]).astype(jnp.bfloat16)
        for e in range(1, NX):
            to = plus(x, e, NX)
            n = d * 3 + e - 1
            bx_copies[d].append(start(remote(
                xback.at[d, to], xret[d].at[x], bxsend_sem.at[n], bxrecv_sem.at[n], at_x(to))))
        xret[d][x] = xback[d, x]

    big[3].wait()
    big[4].wait()

    def add_grams(s):
        held = tbl(T_HELD + s) > 0
        block = gmat[s]
        outer = lax.dot_general(block, block, (((1,), (1,)), ((), ())), preferred_element_type=jnp.float32)
        gl_out[0, 0, s] = gl[s] + jnp.where(held, outer, 0.0)
        outer = lax.dot_general(block, block, (((0,), (0,)), ((), ())), preferred_element_type=jnp.float32)
        gr[s] = gr[s] + jnp.where(held, outer, 0.0)

    pl.loop(0, SLOTS)(add_grams)
    gr_out0[0, 0, 0] = gr[0]
    out_copy = pltpu.make_async_copy(gr.at[1], gr_out1.at[0, 0, 0], osem)
    out_copy.start()

    for d in BACK_ORDER:
        for copy in bx_copies[d]:
            copy.wait_recv()
        land = zback if d else zret
        for k in range(cap):
            e = tbl(T_OWNED + k)
            land[d, k] = xret[d][e // SLOTS, e % SLOTS]
        if d:
            bz_copies.append(start(remote(
                zback.at[d], zret.at[d], bzsend_sem.at[d - 1], bzrecv_sem.at[d - 1], at_z(plus(z, d, NZ)))))
    for copy in forward:
        copy.wait_send()
    out_copy.wait()
    for copies in bx_copies:
        for copy in copies:
            copy.wait_send()
    for copy in bz_copies:
        copy.wait()
    for j in range(BLOCKS):
        away = (z + NZ - tbl(T_PLANE + j)) % NZ
        upd[0, j] = zret[away, tbl(T_RANK + j)]


def step(cap, collective_id, tbl, pairs, first, adam_v, gram_left, gram_right, root_left, root_right):
    tile = (ROWS, COLS)
    bf, f32 = jnp.bfloat16, jnp.float32
    vm = pltpu.VMEM
    dma = pltpu.SemaphoreType.DMA
    scratch = (
        [vm((BLOCKS,) + tile, bf)] * PARTS
        + [vm((NZ, cap) + tile, bf)] * PARTS
        + [vm((NZ, cap) + tile, bf)] * PARTS
        + [vm((NX, SLOTS, ROWS, ORDER), bf)] * NZ
        + [
            vm((PARTS - 1, BLOCKS) + tile, bf),
            vm((PARTS - 1, NY - 1, BLOCKS) + tile, bf),
            vm((PARTS, BLOCKS) + tile, f32),
            vm((PARTS, NX, SLOTS, NZ) + tile, bf),
            vm((PARTS, NX, SLOTS, NZ) + tile, bf),
            vm((SLOTS, ORDER, ORDER), bf),
            vm((SLOTS, NX, NZ, ROWS, ORDER), f32),
            vm((NZ, NX, SLOTS, ROWS, ORDER), bf),
            vm((NZ, cap, ROWS, ORDER), bf),
            vm((NZ, cap, ROWS, ORDER), bf),
            vm((BLOCKS, ROWS, ORDER), f32),
            vm((SLOTS, ORDER, ORDER), f32),
            vm((SLOTS, ORDER, ORDER), f32),
            vm((SLOTS, ORDER, ORDER), bf),
            vm((SLOTS, ORDER, ORDER), bf),
            vm((BLOCKS, COLS), f32),
            vm((NZ - 1, BLOCKS, COLS), f32),
            vm((BLOCKS, COLS), f32),
            vm((NX - 1, BLOCKS, COLS), f32),
            pltpu.SMEM((8, 128), jnp.int32),
            dma((6,)), dma((PARTS,)),
            dma((PARTS * 3 - 3,)), dma((PARTS * 3 - 3,)),
            dma((PARTS * 7,)), dma((PARTS * 7,)),
            dma((PARTS * 3 + 3,)), dma((PARTS * 3 + 3,)),
            dma((NZ * 3,)), dma((NZ * 3,)),
            dma((NZ - 1,)), dma((NZ - 1,)),
            dma((10,)), dma((10,)), dma,
        ]
    )
    hbm = pl.BlockSpec(memory_space=pl.ANY)
    return pl.pallas_call(
        functools.partial(step_kernel, cap),
        out_shape=(
            pltpu.VMEM((1, BLOCKS, ROWS, ORDER), bf),
            pltpu.VMEM(gram_left.shape, f32),
            pltpu.VMEM((1, 1, 1, ORDER, ORDER), f32),
            jax.ShapeDtypeStruct((1, 1, 1, ORDER, ORDER), f32),
        ),
        in_specs=[hbm] * 8,
        out_specs=(pl.BlockSpec(memory_space=pltpu.VMEM),) * 3 + (hbm,),
        scratch_shapes=scratch,
        compiler_params=pltpu.CompilerParams(
            collective_id=collective_id, has_side_effects=True, vmem_limit_bytes=32 << 20
        ),
        name=f"step_{cap}",
    )(tbl, pairs, first, adam_v, gram_left, gram_right, root_left, root_right)


def place_kernel(upd, gl, gr0, gr1, upd_out, gl_out, gr_out, held, in_sem, sems):
    load = pltpu.make_async_copy(gr1.at[0, 0, 0], held, in_sem)
    load.start()
    pairs = [(gl, gl_out), (gr0.at[0, 0, 0], gr_out.at[0, 0, 0]), (upd, upd_out), (held, gr_out.at[0, 0, 1])]
    copies = []
    for i, (src, dst) in enumerate(pairs):
        if i == 3:
            load.wait()
        copy = pltpu.make_async_copy(src, dst, sems.at[i])
        copy.start()
        copies.append(copy)
    for copy in copies:
        copy.wait()


def place(upd, gl, gr0, gr1):
    hbm = pl.BlockSpec(memory_space=pl.ANY)
    return pl.pallas_call(
        place_kernel,
        out_shape=tuple(jax.ShapeDtypeStruct(a.shape, a.dtype) for a in (upd, gl, gl)),
        in_specs=[hbm] * 4,
        out_specs=(hbm,) * 3,
        scratch_shapes=[
            pltpu.VMEM((ORDER, ORDER), jnp.float32),
            pltpu.SemaphoreType.DMA,
            pltpu.SemaphoreType.DMA((4,)),
        ],
        compiler_params=pltpu.CompilerParams(vmem_limit_bytes=8 << 20),
        name="place",
    )(upd, gl, gr0, gr1)


def per_device(grad_part, adam_v, owner_of, gram_left, gram_right, root_left, root_right):
    by_core = grad_part.reshape((NY, 2) + grad_part.shape[2:])
    pairs, first, table, which = pair_sum(by_core, owner_of.reshape(BLOCKS))
    operands = (table, pairs, first, adam_v, gram_left, gram_right, root_left, root_right)
    branches = [functools.partial(step, cap, i + 1) for i, cap in enumerate(CAPS)]
    return place(*lax.switch(which[0], branches, *operands))


def solution(mesh):
    placed = (
        P("grp", None, None, "fsdp", None),
        P("grp", None, "fsdp", None),
        P("grp", None, None),
        P("grp", "fsdp", None, None, None),
        P("grp", "fsdp", None, None, None),
        P("grp", "fsdp", None, None, None),
        P("grp", "fsdp", None, None, None),
    )
    return jax.shard_map(
        per_device,
        mesh=mesh,
        in_specs=placed,
        out_specs=(
            P("grp", None, "fsdp", None),
            P("grp", "fsdp", None, None, None),
            P("grp", "fsdp", None, None, None),
        ),
        check_vma=False,
    )
```

```python
import functools

import jax
import jax.numpy as jnp
from jax import lax
from jax.experimental import pallas as pl
from jax.experimental.pallas import tpu as pltpu
from jax.sharding import PartitionSpec as P

BETA2 = 0.9
EPS_ADAM = 1e-08
EPS_NORM = 1e-06
MESH = pl.DeviceIdType.MESH

NX, NY, NZ = 4, 4, 8
BLOCKS, ROWS, ORDER, SLOTS = 16, 16, 512, 2
PARTS = 4
COLS = ORDER // PARTS
CAPS = (4, 5, 6, 8)
CHUNKS = 2
BACK_ORDER = (4, 3, 5, 2, 6, 1, 7, 0)

T_LIST, T_PLACE, T_OWNED, T_PLANE, T_RANK, T_MINE, T_HELD = 0, 64, 72, 80, 96, 112, 114


def position():
    g = lax.axis_index("grp")
    f = lax.axis_index("fsdp")
    return g, f, g // 2, g % 2, f // NZ, f % NZ


def remote(src, dst, send, recv, device):
    return pltpu.make_async_remote_copy(
        src_ref=src, dst_ref=dst, send_sem=send, recv_sem=recv,
        device_id=device, device_id_type=MESH,
    )


def block_places(owner_ref):
    shape = (BLOCKS, 128)
    row = lax.broadcasted_iota(jnp.int32, shape, 0)
    lane = lax.broadcasted_iota(jnp.int32, shape, 1)
    down = jnp.zeros(shape, jnp.int32)
    across = jnp.zeros(shape, jnp.int32)
    for j in range(BLOCKS):
        down = jnp.where(row == j, owner_ref[j], down)
        across = jnp.where(lane == j, owner_ref[j], across)
    count = lambda same: jnp.sum(jnp.where(same & (lane < row), 1.0, 0.0), axis=1, keepdims=True)
    slot = count(down == across).astype(jnp.int32)
    ranks = count(down % NZ == across % NZ)
    return down, slot, ranks.astype(jnp.int32), jnp.max(ranks, keepdims=True) + 1.0


def index_table(down, slot, rank, me, z):
    shape = (BLOCKS, 128)
    row = lax.broadcasted_iota(jnp.int32, shape, 0)
    lane = lax.broadcasted_iota(jnp.int32, shape, 1)
    plane, line = down % NZ, down // NZ
    here = plane == z
    mine = down == me
    whole = jnp.zeros(shape, jnp.int32)
    for first, size, cond, value in (
        (T_LIST, 64, lambda e: (plane == e // 8) & (rank == e % 8), row),
        (T_PLACE, 8, lambda e: here & (line == e // SLOTS) & (slot == e % SLOTS), rank),
        (T_OWNED, 8, lambda e: here & (rank == e), line * SLOTS + slot),
        (T_PLANE, 16, lambda e: row == e, plane),
        (T_RANK, 16, lambda e: row == e, rank),
        (T_MINE, 2, lambda e: mine & (slot == e), row),
        (T_HELD, 2, lambda e: mine & (slot == e), 1),
    ):
        entry = lane - first
        whole += jnp.where((entry >= 0) & (entry < size) & cond(entry), value, 0)
    return jnp.sum(whole.astype(jnp.float32), axis=0, keepdims=True).astype(jnp.int32)


def pair_kernel(parts_ref, owner_hbm, out_ref, first_ref, tbl_ref, which_hbm,
                owner_ref, which_ref, small_sem, own, other, pair, yrecv, load, loads, own_sem, send, recv, lsend, lrecv, ysend, yrecv_sem):
    g, f, y, c, x, z = position()
    owner_copy = pltpu.make_async_copy(owner_hbm, owner_ref, small_sem.at[0])
    owner_copy.start()
    barrier = pltpu.get_barrier_semaphore()
    for d in range(1, 8):
        pl.semaphore_signal(barrier, inc=1, device_id=((g + d) % 8, f), device_id_type=MESH)
    own_copies = []
    for p in range(PARTS):
        cols = pl.ds(p * COLS, COLS)
        copy = pltpu.make_async_copy(parts_ref.at[:, c, :, :, cols], own.at[p], own_sem.at[p])
        copy.start()
        own_copies.append(copy)
    owner_copy.wait()
    down, slot, rank, most = block_places(owner_ref)
    load[...] = jnp.broadcast_to(most, (8, 128))
    pl.semaphore_wait(barrier, 7)
    copies = []
    for p in range(PARTS):
        cols = pl.ds(p * COLS, COLS)
        copy = remote(parts_ref.at[:, 1 - c, :, :, cols], other.at[p], send.at[p], recv.at[p], (y * 2 + 1 - c, f))
        copy.start()
        copies.append(copy)
    load_copies = []
    for d in range(1, 8):
        copy = remote(load, loads.at[d], lsend.at[d], lrecv.at[d], ((g + d) % 8, f))
        copy.start()
        load_copies.append(copy)
    own_copies[0].wait()
    copies[0].wait_recv()
    pair[...] = own[0] + other[0]
    y_copies = []
    for d in range(1, NY):
        to = (y + d) % NY
        copy = remote(pair.at[to], yrecv.at[d - 1], ysend.at[d - 1], yrecv_sem.at[d - 1], (to * 2 + c, f))
        copy.start()
        y_copies.append(copy)
    tbl_ref[...] = jnp.broadcast_to(index_table(down, slot, rank, f, z), (8, 128))
    for p in range(1, PARTS):
        own_copies[p].wait()
        copies[p].wait_recv()
        out_ref[p - 1] = own[p] + other[p]
    most = load[...]
    for d in range(1, 8):
        load_copies[d - 1].wait_recv()
        most = jnp.maximum(most, loads[d])
    most = jnp.max(most)
    which_ref[0] = sum((most > cap).astype(jnp.int32) for cap in CAPS[:-1])
    which_copy = pltpu.make_async_copy(which_ref, which_hbm, small_sem.at[1])
    which_copy.start()
    for copy in load_copies + copies:
        copy.wait_send()
    total = pair[y].astype(jnp.float32)
    for d in range(NY - 1):
        y_copies[d].wait_recv()
        total = total + yrecv[d].astype(jnp.float32)
    first_ref[...] = total
    which_copy.wait()
    for copy in y_copies:
        copy.wait_send()


def pair_sum(grad_part, owner_ids):
    part = (BLOCKS, ROWS, COLS)
    vmem = pl.BlockSpec(memory_space=pltpu.VMEM)
    hbm = pl.BlockSpec(memory_space=pl.ANY)
    return pl.pallas_call(
        pair_kernel,
        out_shape=(
            jax.ShapeDtypeStruct((PARTS - 1, NY) + part, jnp.bfloat16),
            jax.ShapeDtypeStruct(part, jnp.float32),
            jax.ShapeDtypeStruct((8, 128), jnp.int32),
            jax.ShapeDtypeStruct((1,), jnp.int32),
        ),
        in_specs=[hbm, hbm],
        out_specs=(vmem, vmem, vmem, hbm),
        scratch_shapes=[
            pltpu.SMEM((BLOCKS,), jnp.int32),
            pltpu.SMEM((1,), jnp.int32),
            pltpu.SemaphoreType.DMA((2,)),
            pltpu.VMEM((PARTS, NY) + part, jnp.bfloat16),
            pltpu.VMEM((PARTS, NY) + part, jnp.bfloat16),
            pltpu.VMEM((NY,) + part, jnp.bfloat16),
            pltpu.VMEM((NY - 1,) + part, jnp.bfloat16),
            pltpu.VMEM((8, 128), jnp.float32),
            pltpu.VMEM((8, 8, 128), jnp.float32),
            pltpu.SemaphoreType.DMA((PARTS,)),
            pltpu.SemaphoreType.DMA((PARTS,)),
            pltpu.SemaphoreType.DMA((PARTS,)),
            pltpu.SemaphoreType.DMA((8,)),
            pltpu.SemaphoreType.DMA((8,)),
            pltpu.SemaphoreType.DMA((NY - 1,)),
            pltpu.SemaphoreType.DMA((NY - 1,)),
        ],
        compiler_params=pltpu.CompilerParams(
            collective_id=0, has_side_effects=True, vmem_limit_bytes=60 << 20
        ),
        name="pair_sum",
    )(grad_part, owner_ids)


def step_kernel(cap, tbl_hbm, pairs, first, adam_hbm, gl_hbm, gr_hbm, rl_hbm, rr_hbm,
                upd, gl_out, gr_out0, gr_out1, *scratch):
    scratch = list(scratch)
    take = lambda n: [scratch.pop(0) for _ in range(n)]
    gbf, zsend, zrecv = (take(PARTS) for _ in range(3))
    xret = take(NZ)
    (yown, yrecv, gsum, xsend, xrecv, gmat, dirb, xback, zback, zret, adam, gl, gr, rl, rr,
     gpart, gzrecv, gzsum, gxrecv, tbls,
     lsem, ysem, ysend_sem, yrecv_sem, zsend_sem, zrecv_sem, xsend_sem, xrecv_sem,
     bxsend_sem, bxrecv_sem, bzsend_sem, bzrecv_sem, gsend_sem, grecv_sem, osem) = scratch
    g, f, y, c, x, z = position()
    at_y = lambda i: (i * 2 + c, f)
    at_z = lambda i: (g, x * NZ + i)
    at_x = lambda i: (g, i * NZ + z)
    plus = lambda a, d, n: (a + d) % n
    sends = []

    def start(copy):
        copy.start()
        sends.append(copy)
        return copy

    barrier = pltpu.get_barrier_semaphore()
    partners = (
        [at_y(plus(y, d, NY)) for d in range(1, NY)]
        + [at_z(plus(z, d, NZ)) for d in range(1, NZ)]
        + [at_x(plus(x, d, NX)) for d in range(1, NX)]
    )
    for partner in partners:
        pl.semaphore_signal(barrier, inc=1, device_id=partner, device_id_type=MESH)
    own_copies = []
    copy = pltpu.make_async_copy(first, gsum.at[0], ysem.at[0])
    copy.start()
    own_copies.append(copy)
    for p in range(1, PARTS):
        copy = pltpu.make_async_copy(pairs.at[p - 1, y], yown.at[p - 1], ysem.at[p])
        copy.start()
        own_copies.append(copy)
    big = []
    for i, (src, dst) in enumerate(((adam_hbm.at[0], adam), (rl_hbm.at[0, 0], rl), (rr_hbm.at[0, 0], rr),
                                    (gl_hbm.at[0, 0], gl), (gr_hbm.at[0, 0], gr), (tbl_hbm, tbls))):
        copy = pltpu.make_async_copy(src, dst, lsem.at[i])
        if i not in (3, 4):
            copy.start()
        big.append(copy)

    y_copies = [[] for _ in range(PARTS)]

    def exchange(p):
        for d in range(1, NY):
            to = plus(y, d, NY)
            n = (p - 1) * 3 + d - 1
            y_copies[p].append(start(remote(
                pairs.at[p - 1, to], yrecv.at[p - 1, d - 1], ysend_sem.at[n], yrecv_sem.at[n], at_y(to))))

    z_copies = [[] for _ in range(PARTS)]
    x_copies = [[] for _ in range(PARTS + 1)]

    def tbl(i):
        return tbls[0, i]

    def reduce_part(p):
        own_copies[p].wait()
        for copy in y_copies[p]:
            copy.wait_recv()
        if p == 0:
            gbf[p][...] = gsum[p].astype(jnp.bfloat16)
        else:
            total = yown[p - 1].astype(jnp.float32)
            for d in range(NY - 1):
                total = total + yrecv[p - 1, d].astype(jnp.float32)
            gsum[p] = total
            gbf[p][...] = total.astype(jnp.bfloat16)

        @pl.loop(0, NZ)
        def _(i):
            for k in range(cap):
                zsend[p][i, k] = gbf[p][tbl(T_LIST + i * 8 + k)]

    def send_part(p):
        for d in range(1, NZ):
            to = plus(z, d, NZ)
            n = p * 7 + d - 1
            z_copies[p].append(start(remote(
                zsend[p].at[to], zrecv[p].at[z], zsend_sem.at[n], zrecv_sem.at[n], at_z(to))))
        zrecv[p][z] = zsend[p][z]

    def pass_on(p):
        for copy in z_copies[p]:
            copy.wait_recv()

        def pick(to, s):
            k = tbl(T_PLACE + to * SLOTS + s)
            for r in range(NZ):
                xsend[p, to, s, r] = zrecv[p][r, k]

        if p < PARTS - 1:
            for d in range(1, NX):
                to = plus(x, d, NX)
                n = p * 3 + d - 1
                for s in range(SLOTS):
                    pick(to, s)
                x_copies[p].append(start(remote(
                    xsend.at[p, to], xrecv.at[p, x], xsend_sem.at[n], xrecv_sem.at[n], at_x(to))))
        else:
            for s in range(SLOTS):
                for d in range(1, NX):
                    to = plus(x, d, NX)
                    n = (p + s) * 3 + d - 1
                    pick(to, s)
                    x_copies[p + s].append(start(remote(
                        xsend.at[p, to, s], xrecv.at[p, x, s], xsend_sem.at[n], xrecv_sem.at[n], at_x(to))))
        for s in range(SLOTS):
            pick(x, s)
        xrecv[p, x] = xsend[p, x]

    def apply_roots(p, s):
        block = xrecv[p, :, s].reshape(ORDER, COLS)
        gmat[s, :, p * COLS:(p + 1) * COLS] = block
        left = jnp.dot(rl[s], block, preferred_element_type=jnp.float32).astype(jnp.bfloat16)
        term = jnp.dot(left, rr[s, p * COLS:(p + 1) * COLS, :], preferred_element_type=jnp.float32)
        term = term.reshape(NX, NZ, ROWS, ORDER)
        if p == 0:
            dirb[s] = term
        else:
            dirb[s] += term

    def apply_both(p):
        for copy in x_copies[p]:
            copy.wait_recv()
        pl.loop(0, SLOTS)(lambda s: apply_roots(p, s))

    graft_z = []
    graft_x = []

    def graft_first():
        big[0].wait()
        part = jnp.zeros((BLOCKS, COLS), jnp.float32)
        for p in range(PARTS):
            total = gsum[p]
            second = BETA2 * adam[:, :, p * COLS:(p + 1) * COLS] + (1.0 - BETA2) * total * total
            ratio = total / (jnp.sqrt(second) + EPS_ADAM)
            part = part + jnp.sum(ratio * ratio, axis=1)
        gpart[...] = part
        for d in range(1, NZ):
            graft_z.append(start(remote(
                gpart, gzrecv.at[d - 1], gsend_sem.at[d - 1], grecv_sem.at[d - 1], at_z(plus(z, d, NZ)))))

    def graft_second():
        total = gpart[...]
        for d in range(NZ - 1):
            graft_z[d].wait_recv()
            total = total + gzrecv[d]
        gzsum[...] = total
        for d in range(1, NX):
            n = 6 + d
            graft_x.append(start(remote(
                gzsum, gxrecv.at[d - 1], gsend_sem.at[n], grecv_sem.at[n], at_x(plus(x, d, NX)))))

    big[5].wait()
    reduce_part(0)
    pl.semaphore_wait(barrier, len(partners))
    exchange(1)
    send_part(0)
    for p in range(2, PARTS):
        exchange(p)
    reduce_part(1)
    send_part(1)
    pass_on(0)
    reduce_part(2)
    send_part(2)
    pass_on(1)
    reduce_part(3)
    send_part(3)
    big[3].start()
    big[4].start()
    graft_first()
    big[1].wait()
    big[2].wait()
    apply_both(0)
    pass_on(2)
    graft_second()
    apply_both(1)
    pass_on(3)
    apply_both(2)
    graft = gzsum[...]
    for d in range(NX - 1):
        graft_x[d].wait_recv()
        graft = graft + gxrecv[d]
    block_ids = lax.broadcasted_iota(jnp.int32, (BLOCKS, COLS), 0)
    graft_norms = []
    for s in range(SLOTS):
        graft_norms.append(jnp.sqrt(jnp.sum(jnp.where(block_ids == tbl(T_MINE + s), graft, 0.0), keepdims=True)))
    scales = []
    for s in range(SLOTS):
        for copy in x_copies[PARTS - 1 + s]:
            copy.wait_recv()
        apply_roots(PARTS - 1, s)
        whole = dirb[s]
        norm = jnp.sqrt(jnp.sum((whole * whole).reshape(ORDER, ORDER), keepdims=True))
        scales.append(-(graft_norms[s] / (norm + EPS_NORM)))
    forward = list(sends)
    bx_copies = [[] for _ in range(NZ)]
    bz_copies = []
    for d in BACK_ORDER:
        plane = plus(z, d, NZ)
        for s in range(SLOTS):
            xback[d, :, s] = (dirb[s, :, plane] * scales[s]).astype(jnp.bfloat16)
        for e in range(1, NX):
            to = plus(x, e, NX)
            n = d * 3 + e - 1
            bx_copies[d].append(start(remote(
                xback.at[d, to], xret[d].at[x], bxsend_sem.at[n], bxrecv_sem.at[n], at_x(to))))
        xret[d][x] = xback[d, x]

    big[3].wait()
    big[4].wait()

    def add_grams(s):
        held = tbl(T_HELD + s) > 0
        block = gmat[s]
        outer = lax.dot_general(block, block, (((1,), (1,)), ((), ())), preferred_element_type=jnp.float32)
        gl_out[0, 0, s] = gl[s] + jnp.where(held, outer, 0.0)
        outer = lax.dot_general(block, block, (((0,), (0,)), ((), ())), preferred_element_type=jnp.float32)
        gr[s] = gr[s] + jnp.where(held, outer, 0.0)

    pl.loop(0, SLOTS)(add_grams)
    gr_out0[0, 0, 0] = gr[0]
    out_copy = pltpu.make_async_copy(gr.at[1], gr_out1.at[0, 0, 0], osem)
    out_copy.start()

    for d in BACK_ORDER:
        for copy in bx_copies[d]:
            copy.wait_recv()
        land = zback if d else zret
        for k in range(cap):
            e = tbl(T_OWNED + k)
            land[d, k] = xret[d][e // SLOTS, e % SLOTS]
        if d:
            bz_copies.append(start(remote(
                zback.at[d], zret.at[d], bzsend_sem.at[d - 1], bzrecv_sem.at[d - 1], at_z(plus(z, d, NZ)))))
    for copy in forward:
        copy.wait_send()
    out_copy.wait()
    for copies in bx_copies:
        for copy in copies:
            copy.wait_send()
    for copy in bz_copies:
        copy.wait()
    for j in range(BLOCKS):
        away = (z + NZ - tbl(T_PLANE + j)) % NZ
        upd[0, j] = zret[away, tbl(T_RANK + j)]


def step(cap, collective_id, tbl, pairs, first, adam_v, gram_left, gram_right, root_left, root_right):
    tile = (ROWS, COLS)
    bf, f32 = jnp.bfloat16, jnp.float32
    vm = pltpu.VMEM
    dma = pltpu.SemaphoreType.DMA
    scratch = (
        [vm((BLOCKS,) + tile, bf)] * PARTS
        + [vm((NZ, cap) + tile, bf)] * PARTS
        + [vm((NZ, cap) + tile, bf)] * PARTS
        + [vm((NX, SLOTS, ROWS, ORDER), bf)] * NZ
        + [
            vm((PARTS - 1, BLOCKS) + tile, bf),
            vm((PARTS - 1, NY - 1, BLOCKS) + tile, bf),
            vm((PARTS, BLOCKS) + tile, f32),
            vm((PARTS, NX, SLOTS, NZ) + tile, bf),
            vm((PARTS, NX, SLOTS, NZ) + tile, bf),
            vm((SLOTS, ORDER, ORDER), bf),
            vm((SLOTS, NX, NZ, ROWS, ORDER), f32),
            vm((NZ, NX, SLOTS, ROWS, ORDER), bf),
            vm((NZ, cap, ROWS, ORDER), bf),
            vm((NZ, cap, ROWS, ORDER), bf),
            vm((BLOCKS, ROWS, ORDER), f32),
            vm((SLOTS, ORDER, ORDER), f32),
            vm((SLOTS, ORDER, ORDER), f32),
            vm((SLOTS, ORDER, ORDER), bf),
            vm((SLOTS, ORDER, ORDER), bf),
            vm((BLOCKS, COLS), f32),
            vm((NZ - 1, BLOCKS, COLS), f32),
            vm((BLOCKS, COLS), f32),
            vm((NX - 1, BLOCKS, COLS), f32),
            pltpu.SMEM((8, 128), jnp.int32),
            dma((6,)), dma((PARTS,)),
            dma((PARTS * 3 - 3,)), dma((PARTS * 3 - 3,)),
            dma((PARTS * 7,)), dma((PARTS * 7,)),
            dma((PARTS * 3 + 3,)), dma((PARTS * 3 + 3,)),
            dma((NZ * 3,)), dma((NZ * 3,)),
            dma((NZ - 1,)), dma((NZ - 1,)),
            dma((10,)), dma((10,)), dma,
        ]
    )
    hbm = pl.BlockSpec(memory_space=pl.ANY)
    return pl.pallas_call(
        functools.partial(step_kernel, cap),
        out_shape=(
            pltpu.VMEM((1, BLOCKS, ROWS, ORDER), bf),
            pltpu.VMEM(gram_left.shape, f32),
            pltpu.VMEM((1, 1, 1, ORDER, ORDER), f32),
            jax.ShapeDtypeStruct((1, 1, 1, ORDER, ORDER), f32),
        ),
        in_specs=[hbm] * 8,
        out_specs=(pl.BlockSpec(memory_space=pltpu.VMEM),) * 3 + (hbm,),
        scratch_shapes=scratch,
        compiler_params=pltpu.CompilerParams(
            collective_id=collective_id, has_side_effects=True, vmem_limit_bytes=32 << 20
        ),
        name=f"step_{cap}",
    )(tbl, pairs, first, adam_v, gram_left, gram_right, root_left, root_right)


def place_kernel(upd, gl, gr0, gr1, upd_out, gl_out, gr_out, held, in_sem, sems):
    load = pltpu.make_async_copy(gr1.at[0, 0, 0], held, in_sem)
    load.start()
    pairs = [(gl, gl_out), (gr0.at[0, 0, 0], gr_out.at[0, 0, 0]), (upd, upd_out), (held, gr_out.at[0, 0, 1])]
    copies = []
    for i, (src, dst) in enumerate(pairs):
        if i == 3:
            load.wait()
        copy = pltpu.make_async_copy(src, dst, sems.at[i])
        copy.start()
        copies.append(copy)
    for copy in copies:
        copy.wait()


def place(upd, gl, gr0, gr1):
    hbm = pl.BlockSpec(memory_space=pl.ANY)
    return pl.pallas_call(
        place_kernel,
        out_shape=tuple(jax.ShapeDtypeStruct(a.shape, a.dtype) for a in (upd, gl, gl)),
        in_specs=[hbm] * 4,
        out_specs=(hbm,) * 3,
        scratch_shapes=[
            pltpu.VMEM((ORDER, ORDER), jnp.float32),
            pltpu.SemaphoreType.DMA,
            pltpu.SemaphoreType.DMA((4,)),
        ],
        compiler_params=pltpu.CompilerParams(vmem_limit_bytes=8 << 20),
        name="place",
    )(upd, gl, gr0, gr1)


def per_device(grad_part, adam_v, owner_of, gram_left, gram_right, root_left, root_right):
    by_core = grad_part.reshape((NY, 2) + grad_part.shape[2:])
    pairs, first, table, which = pair_sum(by_core, owner_of.reshape(BLOCKS))
    operands = (table, pairs, first, adam_v, gram_left, gram_right, root_left, root_right)
    branches = [functools.partial(step, cap, i + 1) for i, cap in enumerate(CAPS)]
    return place(*lax.switch(which[0], branches, *operands))


def solution(mesh):
    placed = (
        P("grp", None, None, "fsdp", None),
        P("grp", None, "fsdp", None),
        P("grp", None, None),
        P("grp", "fsdp", None, None, None),
        P("grp", "fsdp", None, None, None),
        P("grp", "fsdp", None, None, None),
        P("grp", "fsdp", None, None, None),
    )
    return jax.shard_map(
        per_device,
        mesh=mesh,
        in_specs=placed,
        out_specs=(
            P("grp", None, "fsdp", None),
            P("grp", "fsdp", None, None, None),
            P("grp", "fsdp", None, None, None),
        ),
        check_vma=False,
    )
```
